256 devices in a mesh: dp: 4 (over y), expert: 8 (over z), etp: 8 (over x, core).
Axes of the slice: x: 4, y: 4, z: 8, core: 2. Of those that a mesh axis runs over, the one named last changes fastest.
Arguments:
- tokens: bfloat16 [4096, 3072], P(('dp', 'expert')), may hold values from -6 to 6
- grad_out: bfloat16 [4096, 3072], P(('dp', 'expert')), may hold values from -6 to 6
- gate_prob: float32 [4096, 2], P(('dp', 'expert')), may hold values from 0.1 to 1
- expert_ids: int32 [4096, 2], P(('dp', 'expert')), may hold values from 0 to 7, all different within a row; in each aligned block of 128 rows (0 to 127, 128 to 255, ...) at most 36 rows name the same one
- w_gate: bfloat16 [8, 3072, 8192], P('expert', None, ('dp', 'etp')), may hold values from -0.109375 to 0.109375
- w_up: bfloat16 [8, 3072, 8192], P('expert', None, ('dp', 'etp')), may hold values from -0.109375 to 0.109375
- w_down: bfloat16 [8, 8192, 3072], P('expert', ('dp', 'etp')), may hold values from -0.0625 to 0.0625
Outputs:
- grad_tokens: bfloat16 [4096, 3072], P(('dp', 'expert'), 'etp')
- grad_w_gate: bfloat16 [8, 3072, 8192], P('expert', None, ('dp', 'etp'))
- grad_w_up: bfloat16 [8, 3072, 8192], P('expert', None, ('dp', 'etp'))
- grad_w_down: bfloat16 [8, 8192, 3072], P('expert', ('dp', 'etp'))
The draws below stay inside these ranges and needn't reach their ends.
Inputs may be any that keep to these rules, and one draw needn't show every extreme that they name: `expert_ids`: each row names two different experts. Within each aligned block of 128 rows no expert is named by more than 36 rows, a bound that some block reaches.
All inputs are finite; a program needn't handle non-finite values.
Results may differ from the reference program's by a relative error of at most 0.02.
Values may be sent and summed in bfloat16 or wider, within the bound.
No kernel may reach another device: no remote copies, remote signals or barrier semaphores. Data moves between devices by JAX's collectives and lax.ppermute only.
A program may use at most 128 MiB of HBM per device.

```python
import math
import jax
import jax.numpy as jnp
import numpy as np
from jax import lax

D = 3072
FF = 8192
TOK_DEV = 128
EXPERTS = 8
CAP = 36
TOKENS = 4096
N_DP = 4
N_EXPERT = 8
N_ETP = 8


def level_of(own_key, shape, split, smallest, high):
    factor_of = 1.0
    for axis_at, shards_of in split:
        draws = jax.random.uniform(jax.random.fold_in(jax.random.fold_in(own_key, 6), axis_at), (shards_of,), jnp.float32, smallest / len(split), high / len(split))
        factor_of = factor_of * jnp.repeat(jnp.exp(draws), shape[axis_at] // shards_of).reshape((-1,) + (1,) * (len(shape) - 1 - axis_at))
    return factor_of


def shared_out(key, own, number, rows, amount, top, limit, lean):
    sequence = jax.random.permutation(key, amount)
    crowded, ordinary = portions_of(amount, rows * top, limit, lean, True), portions_of(amount, rows * top, limit, lean, False)
    places = jnp.arange(amount)

    def named(tallies, rotation):
        used = int((tallies > 0).sum())
        fixed = max(1, used // 4)
        passed = fixed + (places - fixed + rotation * (used - fixed)) % max(1, amount - fixed)
        return jnp.zeros((amount,), jnp.int32).at[sequence[jnp.where(places < fixed, places, passed)]].set(jnp.asarray(tallies, jnp.int32))

    tallies = jnp.where(number % 4 == 0, named(crowded, number // 4), named(ordinary, number - number // 4 - 1))
    mixed = jax.random.permutation(jax.random.fold_in(own, 3), amount)
    giver, sink = mixed[0:amount // 2 * 2:2], mixed[1:amount // 2 * 2:2]
    margin = jnp.minimum(tallies[giver] - 1, limit - tallies[sink]) // 2
    margin = jnp.where((giver == sequence[0]) | (sink == sequence[0]) | (tallies[sink] == 0), 0, jnp.maximum(margin, 0))
    passed = jax.random.randint(jax.random.fold_in(own, 4), (amount // 2,), 0, 1 << 20) % (margin + 1)
    tallies = tallies.at[giver].add(-passed).at[sink].add(passed)
    items = jnp.searchsorted(jnp.cumsum(tallies), jnp.arange(rows * top), side="right").astype(jnp.int32)
    listing = items.reshape(top, rows).T
    listing = listing[jax.random.permutation(jax.random.fold_in(own, 1), rows)]
    rotation = jax.random.randint(jax.random.fold_in(own, 2), (rows, 1), 0, top)
    return jnp.take_along_axis(listing, (jnp.arange(top)[None, :] + rotation) % top, axis=1)


def portions_of(number_of, total, bound, lean, full):
    portions = [(1 << 20) // math.isqrt(standing ** lean) + 1 for standing in range(1, number_of + 1)]
    largest = bound if full else min(bound, max(-(-total // number_of), total * portions[0] // sum(portions)))
    least = 1 if total - largest >= number_of - 1 else 0
    holding, surplus = [largest] + [least] * (number_of - 1), total - largest - least * (number_of - 1)
    while surplus > 0:
        movable = [i for i in range(1, number_of) if holding[i] < largest] or [i for i in range(1, number_of) if holding[i] < bound]
        mass, remaining = sum([portions[i] for i in movable]), surplus
        for i in movable:
            addition = min(bound - holding[i], max(1, remaining * portions[i] // mass), surplus)
            holding[i] = holding[i] + addition
            surplus = surplus - addition
    return np.array(holding)


def centred(own_key, extent, deviation, limit, cuts=(), kind=jnp.bfloat16):
    result = jax.random.normal(own_key, extent, jnp.float32) * deviation
    if len(cuts) > 0:
        result = level_of(own_key, extent, cuts, -0.22, 0.18) * result
    return jnp.clip(result, min=-limit, max=limit).astype(kind)


def setup_inputs(seed: int = 0) -> dict:
    streams_of = jax.random.split(jax.random.key(seed), 8)
    tokens = centred(streams_of[0], (TOKENS, D), 1.0, 6.0, ((0, 32),))
    grad_out = centred(streams_of[1], (TOKENS, D), 1.0, 6.0, ((0, 32),))
    gate_prob = jnp.clip(0.1 + 0.9 * jax.random.uniform(streams_of[2], (TOKENS, 2), jnp.float32) ** level_of(streams_of[2], (TOKENS, 2), ((0, 32),), -0.2, 0.2), 0.1, 1.0)
    expert_ids_keys = jax.random.split(jax.random.fold_in(streams_of[3], 1), TOKENS // TOK_DEV)
    expert_ids_turns = jax.random.permutation(jax.random.fold_in(streams_of[3], 3), TOKENS // TOK_DEV)
    expert_ids = jax.vmap(lambda own, number: shared_out(jax.random.fold_in(streams_of[3], 2), own, number, TOK_DEV, EXPERTS, 2, CAP, 1))(expert_ids_keys, expert_ids_turns).reshape((TOKENS, 2))
    w_gate = centred(streams_of[4], (EXPERTS, D, FF), D ** -0.5, 0.109375, ((0, 8), (2, 32)))
    w_up = centred(streams_of[5], (EXPERTS, D, FF), D ** -0.5, 0.109375, ((0, 8), (2, 32)))
    w_down = centred(streams_of[6], (EXPERTS, FF, D), FF ** -0.5, 0.0625, ((0, 8), (1, 32)))
    return {"tokens": tokens, "grad_out": grad_out, "gate_prob": gate_prob, "expert_ids": expert_ids, "w_gate": w_gate, "w_up": w_up, "w_down": w_down}


def expert_grads(inputs):
    x_rows, y_rows, gate_w, up_w, down_w = inputs
    hidden_h = jnp.dot(x_rows, gate_w, preferred_element_type=jnp.float32)
    hidden_u = jnp.dot(x_rows, up_w, preferred_element_type=jnp.float32)
    sigmoid_h = jax.nn.sigmoid(hidden_h)
    silu_h = hidden_h * sigmoid_h
    act_bf = (silu_h * hidden_u).astype(jnp.bfloat16)
    grad_a = jnp.dot(y_rows, down_w.T, preferred_element_type=jnp.float32)
    grad_h = (grad_a * hidden_u * (sigmoid_h * (1.0 + hidden_h * (1.0 - sigmoid_h)))).astype(jnp.bfloat16)
    grad_u = (grad_a * silu_h).astype(jnp.bfloat16)
    gw_gate = jnp.dot(x_rows.T, grad_h, preferred_element_type=jnp.float32).astype(jnp.bfloat16)
    gw_up = jnp.dot(x_rows.T, grad_u, preferred_element_type=jnp.float32).astype(jnp.bfloat16)
    gw_down = jnp.dot(act_bf.T, y_rows, preferred_element_type=jnp.float32).astype(jnp.bfloat16)
    groups = N_DP * N_ETP
    group_size = FF // groups

    def split_groups(matrix):
        return jnp.moveaxis(matrix.reshape(matrix.shape[0], groups, group_size), 1, 0)

    def add_group(accum_dx, pieces):
        gh_part, gu_part, wg_part, wu_part = pieces
        summed = jnp.dot(gh_part, wg_part.T, preferred_element_type=jnp.float32)
        summed = summed + jnp.dot(gu_part, wu_part.T, preferred_element_type=jnp.float32)
        summed = lax.optimization_barrier(summed.astype(jnp.bfloat16)).astype(jnp.float32)
        return accum_dx + summed, None

    start_dx = jnp.zeros((x_rows.shape[0], D), jnp.float32)
    total_dx, _ = lax.scan(add_group, start_dx, (split_groups(grad_h), split_groups(grad_u), split_groups(gate_w), split_groups(up_w)))
    return gw_gate, gw_up, gw_down, total_dx


def reference(tokens, grad_out, gate_prob, expert_ids, w_gate, w_up, w_down):
    blocks = N_DP * N_EXPERT
    flat_ids = expert_ids.reshape(blocks, TOK_DEV * 2).astype(jnp.int32)
    one_hot = (flat_ids[:, :, None] == jnp.arange(EXPERTS, dtype=jnp.int32)[None, None, :]).astype(jnp.int32)
    before_count = jnp.cumsum(one_hot, axis=1) - one_hot
    slot_pos = jnp.sum(before_count * one_hot, axis=2).astype(jnp.int32)
    block_index = jnp.arange(blocks, dtype=jnp.int32)[:, None]
    dest_index = ((flat_ids * blocks + block_index) * CAP + slot_pos).reshape(-1).astype(jnp.int32)
    x_copies = jnp.repeat(tokens, 2, axis=0)
    y_copies = (gate_prob.reshape(-1)[:, None] * jnp.repeat(grad_out, 2, axis=0).astype(jnp.float32)).astype(jnp.bfloat16)
    total_slots = EXPERTS * blocks * CAP
    x_slots = jnp.zeros((total_slots, D), jnp.bfloat16).at[dest_index].set(x_copies).reshape(EXPERTS, blocks * CAP, D)
    y_slots = jnp.zeros((total_slots, D), jnp.bfloat16).at[dest_index].set(y_copies).reshape(EXPERTS, blocks * CAP, D)
    gw_gate, gw_up, gw_down, slot_dx = lax.map(expert_grads, (x_slots, y_slots, w_gate, w_up, w_down))
    picked = slot_dx.reshape(total_slots, D)[dest_index]
    grad_tokens = jnp.sum(picked.reshape(TOKENS, 2, D), axis=1).astype(jnp.bfloat16)
    return grad_tokens, gw_gate, gw_up, gw_down
```

```python
import jax
import jax.numpy as jnp
from jax import lax
from jax.sharding import Mesh, PartitionSpec as P

BF = jnp.bfloat16
F32 = jnp.float32


def turn(a, axis, step):
    size = lax.axis_size(axis)
    return lax.ppermute(a, axis, [(i, (i + step) % size) for i in range(size)])


def swap(a):
    return lax.ppermute(a, "core", [(0, 1), (1, 0)])


def dot(a, b, dims):
    return lax.dot_general(a, b, (dims, ((), ())), preferred_element_type=F32)


def shards(tokens, grad_out, gate_prob, expert_ids, w_gate, w_up, w_down):
    rows, width = tokens.shape
    experts = lax.axis_size("expert")
    nx = lax.axis_size("x")
    capacity = rows * 9 // (4 * experts)
    half = capacity // 2
    cols = width // nx
    xi = lax.axis_index("x")
    core = lax.axis_index("core")

    ids = expert_ids.T
    lanes = jnp.arange(experts, dtype=jnp.int32)[:, None]
    named = [ids[k][None, :] == lanes for k in range(2)]
    member = named[0] | named[1]
    before = (
        jnp.arange(rows, dtype=jnp.int32)[:, None] < jnp.arange(rows, dtype=jnp.int32)[None, :]
    ).astype(BF)
    slot = dot(member.astype(BF), before, ((1,), (0,))).astype(jnp.int32)
    slot = jnp.where(member, slot, -1)
    gates = gate_prob.T
    gate = jnp.where(named[0], gates[0][None, :], 0.0) + jnp.where(
        named[1], gates[1][None, :], 0.0
    )
    mine = core * half + jnp.arange(half, dtype=jnp.int32)
    hit = slot[:, None, :] == mine[None, :, None]
    slot_gate = jnp.sum(jnp.where(hit, gate[:, None, :], 0.0), axis=2).reshape(-1, 1)
    pick = hit.astype(BF).reshape(experts * half, rows)
    every = jnp.arange(capacity, dtype=jnp.int32)
    pick_all = (
        (slot[:, None, :] == every[None, :, None])
        .astype(BF)
        .reshape(experts, 2, half, rows)
        .swapaxes(0, 1)
        .reshape(2 * experts * half, rows)
    )

    tok_cols = lax.dynamic_slice_in_dim(tokens, xi * cols, cols, 1)
    out_cols = lax.dynamic_slice_in_dim(grad_out, xi * cols, cols, 1)
    send_x = dot(pick, tok_cols, ((1,), (0,))).astype(BF).reshape(experts, half, cols)
    send_y = (dot(pick, out_cols, ((1,), (0,))) * slot_gate).astype(BF)
    send_y = send_y.reshape(experts, half, cols)
    sent = jnp.concatenate([send_x, send_y], axis=1)
    got = lax.all_to_all(sent, "expert", split_axis=0, concat_axis=0, tiled=True)
    x0 = got[:, :half].reshape(experts * half, cols)
    y0 = got[:, half:].reshape(experts * half, cols)

    def rolled(w, axis):
        twice = jnp.concatenate([w, w], axis=axis)
        return lax.dynamic_slice_in_dim(twice, xi * cols, width, axis)

    w_gu = rolled(jnp.concatenate([w_gate[0], w_up[0]], axis=1), 0)
    w_d = rolled(w_down[0], 1)
    w_gu2, w_d2 = swap(w_gu), swap(w_d)
    hid = w_d.shape[0]

    xs = [x0, turn(x0, "x", -1), turn(x0, "x", 2), turn(x0, "x", 1)]
    ys = [y0, turn(y0, "dp", -1), turn(y0, "dp", 2), turn(y0, "dp", 1)]
    xrow = jnp.concatenate(xs, axis=1)
    ycol = jnp.concatenate(ys, axis=0)
    x1, x3 = turn(xrow, "dp", -1), turn(xrow, "dp", 1)
    y1, y3 = turn(ycol, "x", -1), turn(ycol, "x", 1)
    hx, hy = xrow.shape[0] // 2, ycol.shape[0] // 2
    x2a, x2b = turn(x1[:hx], "dp", -1), turn(x3[hx:], "dp", 1)
    y2a, y2b = turn(y1[:hy], "x", -1), turn(y3[hy:], "x", 1)

    def hidden(piece):
        return jnp.concatenate(
            [dot(piece, w_gu, ((1,), (0,))), dot(piece, w_gu2, ((1,), (0,)))], axis=1
        )

    hu = jnp.concatenate([hidden(p) for p in (xrow, x1, x2a, x2b, x3)], axis=0)
    h = jnp.concatenate([hu[:, :hid], hu[:, 2 * hid : 3 * hid]], axis=1)
    u = jnp.concatenate([hu[:, hid : 2 * hid], hu[:, 3 * hid :]], axis=1)
    y2 = jnp.concatenate([y2a, y2b], axis=0)
    yall = jnp.concatenate([ycol, y1, y2, y3], axis=1)
    xall = jnp.concatenate([xrow, x1, x2a, x2b, x3], axis=0)
    ga = jnp.concatenate(
        [dot(yall, w_d, ((1,), (1,))), dot(yall, w_d2, ((1,), (1,)))], axis=1
    )
    s = jax.nn.sigmoid(h)
    silu = h * s
    act = (silu * u).astype(BF)
    gh = (ga * u * (s * (1.0 + h * (1.0 - s)))).astype(BF)
    gu = (ga * silu).astype(BF)
    g1 = jnp.concatenate([gh[:, :hid], gu[:, :hid]], axis=1)
    g2 = jnp.concatenate([gh[:, hid:], gu[:, hid:]], axis=1)
    pg = (dot(g1, w_gu, ((1,), (1,))) + dot(g2, w_gu2, ((1,), (1,)))).astype(BF)

    xo, yo = swap(xall), swap(yall)
    go, ao = swap(g2), swap(act[:, hid:])
    gw = (dot(xall, g1, ((0,), (0,))) + dot(xo, go, ((0,), (0,)))).astype(BF)
    gd = (dot(act[:, :hid], yall, ((0,), (0,))) + dot(ao, yo, ((0,), (0,)))).astype(BF)

    def unrolled(w, axis):
        twice = jnp.concatenate([w, w], axis=axis)
        return lax.dynamic_slice_in_dim(twice, (nx - xi) % nx * cols, width, axis)

    gw = unrolled(gw, 0)
    gd = unrolled(gd, 1)

    def scatter(blocks, axis):
        got = [blocks[0].astype(F32)]
        for k in range(1, 4):
            got.append(turn(blocks[k], axis, k).astype(F32))
        return (got[0] + got[1]) + (got[2] + got[3])

    nd = lax.axis_size("dp")
    hr = experts * half // 2
    pg = pg.reshape(nd, 2, hr, width)
    first = scatter([pg[:, 0, :, k * cols : (k + 1) * cols] for k in range(nx)], "x").astype(BF)
    first = scatter([first[k] for k in range(nd)], "dp")
    second = scatter([pg[k, 1] for k in range(nd)], "dp").astype(BF)
    second = scatter([second[:, k * cols : (k + 1) * cols] for k in range(nx)], "x")
    gx = jnp.concatenate([first, second], axis=0).astype(BF)

    back = gx.reshape(experts, half, 2, cols // 2).transpose(0, 2, 1, 3)
    back = back.reshape(experts * 2, half, cols // 2)
    back = lax.all_to_all(back, ("expert", "core"), split_axis=0, concat_axis=0, tiled=True)
    back = back.reshape(experts, 2, half, cols // 2).transpose(1, 0, 2, 3)
    back = back.reshape(2 * experts * half, cols // 2)
    grad_tokens = dot(pick_all, back, ((0,), (0,))).astype(BF)
    return grad_tokens, gw[None, :, :hid], gw[None, :, hid:], gd[None]


def solution(mesh):
    sizes = mesh.devices.shape
    fine = Mesh(
        mesh.devices.reshape(sizes[0], sizes[1], sizes[2] // 2, 2), ("dp", "expert", "x", "core")
    )
    by_token = P(("dp", "expert"), None)
    up = P("expert", None, ("dp", "x", "core"))
    down = P("expert", ("dp", "x", "core"), None)
    return jax.shard_map(
        shards,
        mesh=fine,
        in_specs=(by_token, by_token, by_token, by_token, up, up, down),
        out_specs=(P(("dp", "expert"), ("x", "core")), up, up, down),
        check_vma=False,
    )
```

```python
import jax
import jax.numpy as jnp
from jax import lax
from jax.experimental import pallas as pl
from jax.experimental.pallas import tpu as pltpu
from jax.sharding import Mesh, PartitionSpec as P

BF = jnp.bfloat16
F32 = jnp.float32


def turn(a, axis, step):
    size = lax.axis_size(axis)
    return lax.ppermute(a, axis, [(i, (i + step) % size) for i in range(size)])


def swap(a):
    return lax.ppermute(a, "core", [(0, 1), (1, 0)])


def dot(a, b, dims):
    return lax.dot_general(a, b, (dims, ((), ())), preferred_element_type=F32)


def same(shape):
    return pl.BlockSpec(shape, lambda k, xi: (0,) * len(shape), pipeline_mode=pl.Buffered(1))


def call(body, grid, in_specs, out_specs, out_shape, args, flops, mib, scratch=()):
    return pl.pallas_call(
        body,
        grid_spec=pltpu.PrefetchScalarGridSpec(
            num_scalar_prefetch=1,
            grid=grid,
            in_specs=in_specs,
            out_specs=out_specs,
            scratch_shapes=scratch,
        ),
        out_shape=out_shape,
        compiler_params=pltpu.CompilerParams(
            dimension_semantics=("arbitrary",), vmem_limit_bytes=mib << 20
        ),
        cost_estimate=pl.CostEstimate(flops=int(flops), bytes_accessed=8 << 20, transcendentals=0),
    )(*args)


def pack(xi, own, theirs):
    width, hid = own[0].shape
    cols = width // 4
    up = pl.BlockSpec((cols, hid), lambda k, xi: ((xi[0] + k) % 4, 0))
    down = pl.BlockSpec((hid, cols), lambda k, xi: (0, (xi[0] + k) % 4))

    def body(xi, g1, u1, d1, g2, u2, d2, w, wd):
        for j, ref in enumerate((g1, u1, g2, u2)):
            w[:, j * hid : (j + 1) * hid] = ref[...]
        wd[:hid] = d1[...]
        wd[hid:] = d2[...]

    return call(
        body,
        (4,),
        [up, up, down] * 2,
        [
            pl.BlockSpec((cols, 4 * hid), lambda k, xi: (k, 0)),
            pl.BlockSpec((2 * hid, cols), lambda k, xi: (0, k)),
        ],
        [jax.ShapeDtypeStruct((width, 4 * hid), BF), jax.ShapeDtypeStruct((2 * hid, width), BF)],
        (xi, *own, *theirs),
        width * hid,
        14,
    )


def hidden_part(xi, pieces, w):
    rows, width = pieces[0].shape
    cols = width // 4
    every = rows * len(pieces)

    def body(xi, *refs):
        *xs, w, out = refs
        a = xs[0][...] if len(xs) == 1 else jnp.concatenate([x[...] for x in xs], axis=0)
        part = dot(a, w[...], ((1,), (0,)))
        first = pl.program_id(0) == 0

        @pl.when(first)
        def _():
            out[...] = part

        @pl.when(jnp.logical_not(first))
        def _():
            out[...] += part

    shape = jax.ShapeDtypeStruct((every, w.shape[1]), F32)
    return call(
        body,
        (4,),
        [pl.BlockSpec((rows, cols), lambda k, xi: (0, k))] * len(pieces)
        + [pl.BlockSpec((cols, w.shape[1]), lambda k, xi: (k, 0))],
        same(shape.shape),
        shape,
        (xi, *pieces, w),
        2 * every * width * w.shape[1],
        14,
    )


def down_part(xi, ys, places, wd, so_far=None):
    rows, cols = ys[0].shape
    n = len(ys)
    more = [] if so_far is None else [so_far]

    def body(xi, *refs):
        out = dot(refs[0][...], refs[n][...], ((1,), (1,)))
        for j in range(1, n):
            out += dot(refs[j][...], refs[n + j][...], ((1,), (1,)))
        if more:
            out += refs[2 * n][...]
        refs[-1][...] = out

    shape = jax.ShapeDtypeStruct((rows, wd.shape[0]), F32)
    return call(
        body,
        (1,),
        [same((rows, cols))] * n
        + [pl.BlockSpec((wd.shape[0], cols), lambda k, xi, j=j: (0, j)) for j in places]
        + [same(shape.shape)] * len(more),
        same(shape.shape),
        shape,
        (xi, *ys, *(wd,) * n, *more),
        2 * n * rows * cols * wd.shape[0],
        16,
    )


def token_part(xi, hu0, hu13, ga, x2a, x2b, y2a, y2b, w, wd):
    rows, side = x2a.shape
    width = 2 * side
    cols = width // 4
    hid = w.shape[1] // 4
    every = 4 * rows

    def body(xi, h0, h13, ga1, xa, xb, ya, yb, w, wd, act, g, pa, pb, h2):
        step = pl.program_id(0)

        @pl.when(step < 4)
        def _():
            part = dot(jnp.where(step < 2, xa[...], xb[...]), w[...], ((1,), (0,)))

            @pl.when(step == 0)
            def _():
                h2[...] = part

            @pl.when(step > 0)
            def _():
                h2[...] += part

        @pl.when(step == 3)
        def _():
            y2 = jnp.concatenate([ya[...], yb[...]], axis=0)
            for c in range(2):
                part = slice(c * hid, (c + 1) * hid)
                hs = slice(2 * c * hid, (2 * c + 1) * hid)
                us = slice((2 * c + 1) * hid, (2 * c + 2) * hid)
                ga2 = dot(y2, wd[part, :], ((1,), (1,)))
                for k, (ref, at) in enumerate(((h0, 0), (h13, 0), (h2, 0), (h13, rows))):
                    r = slice(k * rows, (k + 1) * rows)
                    hh = ref[at : at + rows, hs]
                    uu = ref[at : at + rows, us]
                    gg = ga1[r, part] + ga2[r]
                    s = jax.nn.sigmoid(hh)
                    silu = hh * s
                    act[r, part] = (silu * uu).astype(BF)
                    g[r, hs] = (gg * uu * (s * (1.0 + hh * (1.0 - s)))).astype(BF)
                    g[r, us] = (gg * silu).astype(BF)

        @pl.when(step > 3)
        def _():
            out = dot(g[...], w[...], ((1,), (1,))).astype(BF)
            pa[0] = out[:, : cols // 2]
            for k in range(4):
                pb[k] = out[k * rows : (k + 1) * rows, cols // 2 :]

    last = lambda k: jnp.maximum(k - 4, 0)
    shapes = [
        jax.ShapeDtypeStruct((every, 2 * hid), BF),
        jax.ShapeDtypeStruct((every, 4 * hid), BF),
        jax.ShapeDtypeStruct((4, every, cols // 2), BF),
        jax.ShapeDtypeStruct((4, rows, width // 2), BF),
    ]
    return call(
        body,
        (8,),
        [same(a.shape) for a in (hu0, hu13, ga)]
        + [
            pl.BlockSpec((rows, cols), lambda k, xi: (0, jnp.minimum(k, 1))),
            pl.BlockSpec((rows, cols), lambda k, xi: (0, jnp.clip(k - 2, 0, 1))),
            same(y2a.shape),
            same(y2b.shape),
            pl.BlockSpec((cols, 4 * hid), lambda k, xi: (k % 4, 0)),
            pl.BlockSpec((2 * hid, cols), lambda k, xi: (0, 2), pipeline_mode=pl.Buffered(1)),
        ],
        [
            same(shapes[0].shape),
            same(shapes[1].shape),
            pl.BlockSpec((1, every, cols // 2), lambda k, xi: (last(k), 0, 0)),
            pl.BlockSpec((4, rows, cols // 2), lambda k, xi: (0, 0, last(k))),
        ],
        shapes,
        (xi, hu0, hu13, ga, x2a, x2b, y2a, y2b, w, wd),
        2 * every * width * 4 * hid,
        24,
        [pltpu.VMEM((rows, 4 * hid), F32)],
    )


def weight_part(xi, xs, ys, act, g, which):
    xr, x1, x2a, x2b, x3 = xs
    rows, width = xr.shape
    cols = width // 4
    every = 4 * rows
    hid = act.shape[1] // 2
    x_spec = pl.BlockSpec((rows, cols), lambda k, xi: (0, k))
    a_spec = pl.BlockSpec((rows, cols), lambda k, xi: (0, jnp.minimum(k, 1)))
    b_spec = pl.BlockSpec((rows, cols), lambda k, xi: (0, jnp.maximum(k - 2, 0)))

    def body(xi, xrr, x1r, xar, xbr, x3r, y0r, y1r, yar, ybr, y3r, actr, gr, out, ybuf):
        k = pl.program_id(0)
        for j, y in ((0, y0r), (1, y1r), (3, y3r)):

            @pl.when(k == j)
            def _():
                ybuf[...] = y[...]

        @pl.when(k == 2)
        def _():
            ybuf[: every // 2] = yar[...]
            ybuf[every // 2 :] = ybr[...]

        x2 = jnp.where(k < 2, xar[...], xbr[...])
        x = jnp.concatenate([xrr[...], x1r[...], x2, x3r[...]], axis=0)
        out[:, : 2 * hid] = dot(x, gr[...], ((0,), (0,))).astype(BF)
        d = dot(actr[...], ybuf[...], ((0,), (0,))).astype(BF)
        for j in range(cols // hid):
            out[j * hid : (j + 1) * hid, 2 * hid :] = d[:, j * hid : (j + 1) * hid]

    return call(
        body,
        (4,),
        [x_spec, x_spec, a_spec, b_spec, x_spec]
        + [same(y.shape) for y in ys]
        + [
            pl.BlockSpec((every, hid), lambda k, xi: (0, which), pipeline_mode=pl.Buffered(1)),
            pl.BlockSpec((every, 2 * hid), lambda k, xi: (0, which), pipeline_mode=pl.Buffered(1)),
        ],
        pl.BlockSpec((cols, 3 * hid), lambda k, xi: (k, 0)),
        jax.ShapeDtypeStruct((width, 3 * hid), BF),
        (xi, *xs, *ys, act, g),
        2 * 3 * every * width * hid,
        22,
        [pltpu.VMEM((every, cols), BF)],
    )


def weight_sum(xi, mine, rest):
    width = mine.shape[0]
    hid = mine.shape[1] // 3
    cols = width // 4

    def body(xi, a, b, og, ou, od):
        s = (a[...].astype(F32) + b[...].astype(F32)).astype(BF)
        og[...] = s[:, :hid]
        ou[...] = s[:, hid : 2 * hid]
        for j in range(cols // hid):
            c = slice(j * hid, (j + 1) * hid)
            od[:, c] = s[c, 2 * hid :]

    up = pl.BlockSpec((cols, hid), lambda k, xi: ((xi[0] + k) % 4, 0))
    down = pl.BlockSpec((hid, cols), lambda k, xi: (0, (xi[0] + k) % 4))
    part = pl.BlockSpec((cols, 3 * hid), lambda k, xi: (k, 0))
    return call(
        body,
        (4,),
        [part, part],
        [up, up, down],
        [
            jax.ShapeDtypeStruct((width, hid), BF),
            jax.ShapeDtypeStruct((width, hid), BF),
            jax.ShapeDtypeStruct((hid, width), BF),
        ],
        (xi, mine, rest),
        width * hid,
        14,
    )


def add(*parts):
    out = parts[0].astype(F32)
    for p in parts[1:]:
        out = out + p.astype(F32)
    return out.astype(BF)


def tie(values, *late):
    out = lax.optimization_barrier((tuple(values), tuple(late)))
    return out[0]


def shards(tokens, grad_out, gate_prob, expert_ids, w_gate, w_up, w_down):
    rows, width = tokens.shape
    experts = lax.axis_size("expert")
    nx = lax.axis_size("x")
    nd = lax.axis_size("dp")
    capacity = rows * 9 // (4 * experts)
    half = capacity // 2
    cols = width // nx
    xi = lax.axis_index("x")
    core = lax.axis_index("core")
    at = xi.astype(jnp.int32).reshape(1)
    own = (w_gate[0], w_up[0], w_down[0])
    theirs = [swap(w) for w in own]

    ids = expert_ids.T
    lanes = jnp.arange(experts, dtype=jnp.int32)[:, None]
    named = [ids[k][None, :] == lanes for k in range(2)]
    member = named[0] | named[1]
    before = (
        jnp.arange(rows, dtype=jnp.int32)[:, None] < jnp.arange(rows, dtype=jnp.int32)[None, :]
    ).astype(BF)
    slot = dot(member.astype(BF), before, ((1,), (0,))).astype(jnp.int32)
    slot = jnp.where(member, slot, -1)
    gates = gate_prob.T
    gate = jnp.where(named[0], gates[0][None, :], 0.0) + jnp.where(
        named[1], gates[1][None, :], 0.0
    )
    mine = core * half + jnp.arange(half, dtype=jnp.int32)
    hit = slot[:, None, :] == mine[None, :, None]
    slot_gate = jnp.sum(jnp.where(hit, gate[:, None, :], 0.0), axis=2).reshape(-1, 1)
    pick = hit.astype(BF).reshape(experts * half, rows)
    every = jnp.arange(capacity, dtype=jnp.int32)
    pick_all = (
        (slot[:, None, :] == every[None, :, None])
        .astype(BF)
        .reshape(experts, 2, half, rows)
        .swapaxes(0, 1)
        .reshape(2 * experts * half, rows)
    )

    tok_cols = lax.dynamic_slice_in_dim(tokens, xi * cols, cols, 1)
    out_cols = lax.dynamic_slice_in_dim(grad_out, xi * cols, cols, 1)
    send_x = dot(pick, tok_cols, ((1,), (0,))).astype(BF).reshape(experts, half, cols)
    send_y = (dot(pick, out_cols, ((1,), (0,))) * slot_gate).astype(BF)
    send_y = send_y.reshape(experts, half, cols)
    sent = jnp.concatenate([send_x, send_y], axis=1)
    got = lax.all_to_all(sent, "expert", split_axis=0, concat_axis=0, tiled=True)
    w, wd = pack(at, own, theirs)
    (got,) = tie((got,), w, wd)
    x0 = got[:, :half].reshape(experts * half, cols)
    y0 = got[:, half:].reshape(experts * half, cols)
    xs = [x0, turn(x0, "x", -1), turn(x0, "x", 2), turn(x0, "x", 1)]
    ys = [y0, turn(y0, "dp", -1), turn(y0, "dp", 2), turn(y0, "dp", 1)]
    xr = jnp.concatenate(xs, axis=1)
    yc = jnp.concatenate(ys, axis=0)
    x1, x3 = turn(xr, "dp", -1), turn(xr, "dp", 1)
    y1, y3 = turn(yc, "x", -1), turn(yc, "x", 1)
    hu0 = hidden_part(at, (xr,), w)
    ga0 = down_part(at, (yc,), (0,), wd)
    x1, x3, y1, y3 = tie((x1, x3, y1, y3), hu0, ga0)
    hx, hy = width // 2, yc.shape[0] // 2
    x2a, x2b = turn(x1[:, :hx], "dp", -1), turn(x3[:, hx:], "dp", 1)
    y2a, y2b = turn(y1[:hy], "x", -1), turn(y3[hy:], "x", 1)
    hu13 = hidden_part(at, (x1, x3), w)
    ga = down_part(at, (y1, y3), (1, 3), wd, ga0)
    x2a, x2b, y2a, y2b = tie((x2a, x2b, y2a, y2b), hu13, ga)
    act, g, pa, pb = token_part(at, hu0, hu13, ga, x2a, x2b, y2a, y2b, w, wd)

    ra, rb = pa.shape[1] // 2, pb.shape[2] // 2
    a_up, a_dn = turn(pa[2, :ra], "x", 1), turn(pa[2, ra:], "x", -1)
    b_up, b_dn = turn(pb[2, :, :rb], "dp", 1), turn(pb[2, :, rb:], "dp", -1)
    x_all, y_all = (xr, x1, x2a, x2b, x3), (yc, y1, y2a, y2b, y3)
    part = weight_part(at, x_all, y_all, act, g, 1)
    a_up, a_dn, b_up, b_dn, part = tie((a_up, a_dn, b_up, b_dn, part))
    part = swap(part)
    a1 = jnp.concatenate([add(pa[1, :ra], a_up), pa[1, ra:]], axis=0)
    a3 = jnp.concatenate([pa[3, :ra], add(pa[3, ra:], a_dn)], axis=0)
    b1 = jnp.concatenate([add(pb[1, :, :rb], b_up), pb[1, :, rb:]], axis=1)
    b3 = jnp.concatenate([pb[3, :, :rb], add(pb[3, :, rb:], b_dn)], axis=1)
    a1, a3 = turn(a1, "x", 1), turn(a3, "x", -1)
    b1, b3 = turn(b1, "dp", 1), turn(b3, "dp", -1)
    mine = weight_part(at, x_all, y_all, act, g, 0)
    a1, a3, b1, b3 = tie((a1, a3, b1, b3), mine)
    sa = add(pa[0], a1, a3).reshape(nd, -1, cols // 2)
    sb = add(pb[0], b1, b3)
    qa = [turn(sa[k], "dp", k) for k in range(1, nd)]
    qb = [turn(sb[:, k * cols // 2 : (k + 1) * cols // 2], "x", k) for k in range(1, nx)]
    ga_x = add(sa[0], *qa)
    gb_x = add(sb[:, : cols // 2], *qb)

    back = jnp.stack(
        [g.reshape(experts, half, cols // 2) for g in (ga_x, gb_x)], axis=1
    ).reshape(experts * 2, half, cols // 2)
    back = lax.all_to_all(back, ("expert", "core"), split_axis=0, concat_axis=0, tiled=True)
    gw_gate, gw_up, gw_down = weight_sum(at, mine, part)
    (back,) = tie((back,), gw_gate)
    back = back.reshape(experts, 2, half, cols // 2).transpose(1, 0, 2, 3)
    back = back.reshape(2 * experts * half, cols // 2)
    grad_tokens = dot(pick_all, back, ((0,), (0,))).astype(BF)
    return grad_tokens, gw_gate[None], gw_up[None], gw_down[None]


def solution(mesh):
    sizes = mesh.devices.shape
    fine = Mesh(
        mesh.devices.reshape(sizes[0], sizes[1], sizes[2] // 2, 2), ("dp", "expert", "x", "core")
    )
    by_token = P(("dp", "expert"), None)
    up = P("expert", None, ("dp", "x", "core"))
    down = P("expert", ("dp", "x", "core"), None)
    return jax.shard_map(
        shards,
        mesh=fine,
        in_specs=(by_token, by_token, by_token, by_token, up, up, down),
        out_specs=(P(("dp", "expert"), ("x", "core")), up, up, down),
        check_vma=False,
    )
```

```python
import jax
import jax.numpy as jnp
from jax import lax
from jax.experimental import pallas as pl
from jax.experimental.pallas import tpu as pltpu
from jax.sharding import Mesh, PartitionSpec as P

BF = jnp.bfloat16
F32 = jnp.float32


def turn(a, axis, step):
    size = lax.axis_size(axis)
    return lax.ppermute(a, axis, [(i, (i + step) % size) for i in range(size)])


def swap(a):
    return lax.ppermute(a, "core", [(0, 1), (1, 0)])


def ring(a, second, step, cross=False):
    nd, nx = lax.axis_size("dp"), lax.axis_size("x")
    pairs = []
    for d in range(nd):
        for x in range(nx):
            for c in range(2):
                along_x = (c == 0) != second
                to_d, to_x = (d, (x + step) % nx) if along_x else ((d + step) % nd, x)
                to_c = 1 - c if cross else c
                pairs.append(((d * nx + x) * 2 + c, (to_d * nx + to_x) * 2 + to_c))
    return lax.ppermute(a, ("dp", "x", "core"), pairs)


def dot(a, b, dims):
    return lax.dot_general(a, b, (dims, ((), ())), preferred_element_type=F32)


def same(shape):
    return pl.BlockSpec(shape, lambda k, xi: (0,) * len(shape), pipeline_mode=pl.Buffered(1))


def call(body, grid, in_specs, out_specs, out_shape, args, flops, mib, scratch=()):
    return pl.pallas_call(
        body,
        grid_spec=pltpu.PrefetchScalarGridSpec(
            num_scalar_prefetch=1,
            grid=grid,
            in_specs=in_specs,
            out_specs=out_specs,
            scratch_shapes=scratch,
        ),
        out_shape=out_shape,
        compiler_params=pltpu.CompilerParams(
            dimension_semantics=("arbitrary",), vmem_limit_bytes=mib << 20
        ),
        cost_estimate=pl.CostEstimate(flops=int(flops), bytes_accessed=8 << 20, transcendentals=0),
    )(*args)


def dispatch(xi, ids, gates, tokens, grad_out, slots, cols):
    experts = lax.axis_size("expert")
    every, rows = experts * slots, tokens.shape[0]

    def body(xi, ids, gates, tok, grad, sent, pick):
        j = lax.broadcasted_iota(jnp.int32, (every, 1), 0)
        e = jnp.zeros((every, 1), jnp.int32)
        for m in range(1, experts):
            e += (j >= m * slots).astype(jnp.int32)
        s = j - e * slots
        first, second = ids[0:1, :] == e, ids[1:2, :] == e
        member = jnp.where(first | second, 1.0, 0.0)
        early = lax.broadcasted_iota(jnp.int32, (rows, rows), 0)
        late = lax.broadcasted_iota(jnp.int32, (rows, rows), 1)
        before = jnp.where(early < late, 1.0, 0.0).astype(BF)
        slot = dot(member.astype(BF), before, ((1,), (0,)))
        hit = jnp.where(slot == s.astype(F32), member, 0.0)
        gate = jnp.where(first, gates[0:1, :], 0.0) + jnp.where(second, gates[1:2, :], 0.0)
        gate = jnp.sum(hit * gate, axis=1, keepdims=True)
        hit = hit.astype(BF)
        pick[...] = hit

        @pl.when(xi[1] == 0)
        def _():
            sent[...] = dot(hit, tok[...], ((1,), (0,))).astype(BF)

        @pl.when(xi[1] == 1)
        def _():
            sent[...] = (dot(hit, grad[...], ((1,), (0,))) * gate).astype(BF)

    column = pl.BlockSpec((rows, cols), lambda k, xi: (0, xi[0]))
    return call(
        body,
        (1,),
        [same(ids.shape), same(gates.shape), column, column],
        [same((every, cols)), same((every, rows))],
        [jax.ShapeDtypeStruct((every, cols), BF), jax.ShapeDtypeStruct((every, rows), BF)],
        (xi, ids, gates, tokens, grad_out),
        2 * every * rows * cols,
        56,
    )


def row_map(out_rows, in_rows, groups, out_size, in_size):
    r = lax.broadcasted_iota(jnp.int32, (out_rows, in_rows), 0)
    q = lax.broadcasted_iota(jnp.int32, (out_rows, in_rows), 1)
    gr, gq = jnp.zeros_like(r), jnp.zeros_like(q)
    for m in range(1, groups):
        gr += (r >= m * out_size).astype(jnp.int32)
        gq += (q >= m * in_size).astype(jnp.int32)
    match = (gr == gq) & (r - gr * out_size == q - gq * in_size)
    return jnp.where(match, 1.0, 0.0).astype(BF)


def compact(xi, got, groups, capacity):
    rows, cols = got.shape
    every = groups * capacity

    def body(xi, a, out):
        m = row_map(every, rows, groups, capacity, rows // groups)
        out[...] = dot(m, a[...], ((1,), (0,))).astype(BF)

    return call(
        body,
        (1,),
        [same((rows, cols))],
        same((every, cols)),
        jax.ShapeDtypeStruct((every, cols), BF),
        (xi, got),
        2 * every * rows * cols,
        8,
    )


def spread(xi, parts, groups, slots):
    two, half, cols = parts[0].shape
    rows = groups * slots

    def body(xi, *refs):
        *ins, out = refs
        total = ins[0][...].astype(F32)
        for a in ins[1:]:
            total += a[...].astype(F32)
        total = total.astype(BF)
        low = jnp.where(xi[1] == 0, total[0], total[1])
        high = jnp.where(xi[1] == 0, total[1], total[0])
        m = row_map(rows, 2 * half, groups, slots, 2 * half // groups)
        out[...] = dot(m, jnp.concatenate([low, high], axis=0), ((1,), (0,))).astype(BF)

    return call(
        body,
        (1,),
        [same((two, half, cols))] * len(parts),
        same((rows, cols)),
        jax.ShapeDtypeStruct((rows, cols), BF),
        (xi, *parts),
        4 * rows * half * cols,
        8,
    )


def pack(xi, own, theirs):
    width, hid = own[0].shape
    cols = width // 4
    up = pl.BlockSpec((cols, hid), lambda k, xi: ((xi[0] + k) % 4, 0))
    down = pl.BlockSpec((hid, cols), lambda k, xi: (0, (xi[0] + k) % 4))

    def body(xi, g1, u1, d1, g2, u2, d2, w, wd):
        for j, ref in enumerate((g1, u1, g2, u2)):
            w[:, j * hid : (j + 1) * hid] = ref[...]
        wd[:hid] = d1[...]
        wd[hid:] = d2[...]

    return call(
        body,
        (4,),
        [up, up, down] * 2,
        [
            pl.BlockSpec((cols, 4 * hid), lambda k, xi: (k, 0)),
            pl.BlockSpec((2 * hid, cols), lambda k, xi: (0, k)),
        ],
        [jax.ShapeDtypeStruct((width, 4 * hid), BF), jax.ShapeDtypeStruct((2 * hid, width), BF)],
        (xi, *own, *theirs),
        width * hid,
        14,
    )


def hidden_part(xi, pieces, w):
    _, rows, cols = pieces[0].shape
    width = 4 * cols
    every = rows * len(pieces)

    def body(xi, *refs):
        *xs, w, out = refs
        a = xs[0][0] if len(xs) == 1 else jnp.concatenate([x[0] for x in xs], axis=0)
        part = dot(a, w[...], ((1,), (0,)))
        first = pl.program_id(0) == 0

        @pl.when(first)
        def _():
            out[...] = part

        @pl.when(jnp.logical_not(first))
        def _():
            out[...] += part

    shape = jax.ShapeDtypeStruct((every, w.shape[1]), F32)
    return call(
        body,
        (4,),
        [pl.BlockSpec((1, rows, cols), lambda k, xi: (k, 0, 0))] * len(pieces)
        + [pl.BlockSpec((cols, w.shape[1]), lambda k, xi: (k, 0))],
        same(shape.shape),
        shape,
        (xi, *pieces, w),
        2 * every * width * w.shape[1],
        14,
    )


def down_part(xi, ys, places, wd, so_far=None):
    rows, cols = ys[0].shape
    n = len(ys)
    more = [] if so_far is None else [so_far]

    def body(xi, *refs):
        out = dot(refs[0][...], refs[n][...], ((1,), (1,)))
        for j in range(1, n):
            out += dot(refs[j][...], refs[n + j][...], ((1,), (1,)))
        if more:
            out += refs[2 * n][...]
        refs[-1][...] = out

    shape = jax.ShapeDtypeStruct((rows, wd.shape[0]), F32)
    return call(
        body,
        (1,),
        [same((rows, cols))] * n
        + [pl.BlockSpec((wd.shape[0], cols), lambda k, xi, j=j: (0, j)) for j in places]
        + [same(shape.shape)] * len(more),
        same(shape.shape),
        shape,
        (xi, *ys, *(wd,) * n, *more),
        2 * n * rows * cols * wd.shape[0],
        16,
    )


def token_part(xi, hu0, hu13, ga, x2a, x2b, y2a, y2b, w, wd):
    _, rows, cols = x2a.shape
    width = 4 * cols
    hid = w.shape[1] // 4
    every = 4 * rows

    def body(xi, h0, h13, ga1, xa, xb, ya, yb, w, wd, act, g, keep, send, h2):
        step = pl.program_id(0)

        @pl.when(step < 4)
        def _():
            part = dot(jnp.where(step < 2, xa[0], xb[0]), w[...], ((1,), (0,)))

            @pl.when(step == 0)
            def _():
                h2[...] = part

            @pl.when(step > 0)
            def _():
                h2[...] += part

        @pl.when(step == 3)
        def _():
            y2 = jnp.concatenate([ya[...], yb[...]], axis=0)
            for c in range(2):
                part = slice(c * hid, (c + 1) * hid)
                hs = slice(2 * c * hid, (2 * c + 1) * hid)
                us = slice((2 * c + 1) * hid, (2 * c + 2) * hid)
                ga2 = dot(y2, wd[part, :], ((1,), (1,)))
                for k, (ref, at) in enumerate(((h0, 0), (h13, 0), (h2, 0), (h13, rows))):
                    r = slice(k * rows, (k + 1) * rows)
                    hh = ref[at : at + rows, hs]
                    uu = ref[at : at + rows, us]
                    gg = ga1[r, part] + ga2[r]
                    s = jax.nn.sigmoid(hh)
                    silu = hh * s
                    act[r, part] = (silu * uu).astype(BF)
                    g[r, hs] = (gg * uu * (s * (1.0 + hh * (1.0 - s)))).astype(BF)
                    g[r, us] = (gg * silu).astype(BF)

        @pl.when(step > 3)
        def _():
            out = dot(g[...], w[...], ((1,), (1,))).astype(BF)
            for mine, by_x, by_y in ((0, keep, send), (1, send, keep)):

                @pl.when(xi[1] == mine)
                def _():
                    for j in range(4):
                        r = slice(j * rows, (j + 1) * rows)
                        by_x[step - 4, j] = out[r, : cols // 2]
                        by_y[j, step - 4] = out[r, cols // 2 :]

    shapes = [
        jax.ShapeDtypeStruct((every, 2 * hid), BF),
        jax.ShapeDtypeStruct((every, 4 * hid), BF),
        jax.ShapeDtypeStruct((4, 4, rows, cols // 2), BF),
        jax.ShapeDtypeStruct((4, 4, rows, cols // 2), BF),
    ]
    return call(
        body,
        (8,),
        [same(a.shape) for a in (hu0, hu13, ga)]
        + [
            pl.BlockSpec((1, rows, cols), lambda k, xi: (jnp.minimum(k, 1), 0, 0)),
            pl.BlockSpec((1, rows, cols), lambda k, xi: (jnp.clip(k - 2, 0, 1), 0, 0)),
            same(y2a.shape),
            same(y2b.shape),
            pl.BlockSpec((cols, 4 * hid), lambda k, xi: (k % 4, 0)),
            pl.BlockSpec((2 * hid, cols), lambda k, xi: (0, 2), pipeline_mode=pl.Buffered(1)),
        ],
        [same(a.shape) for a in shapes],
        shapes,
        (xi, hu0, hu13, ga, x2a, x2b, y2a, y2b, w, wd),
        2 * every * width * 4 * hid,
        24,
        [pltpu.VMEM((rows, 4 * hid), F32)],
    )


def weight_part(xi, xs, ys, act, g, which, rest=None):
    xr, x1, x2a, x2b, x3 = xs
    _, rows, cols = xr.shape
    width = 4 * cols
    every = 4 * rows
    hid = act.shape[1] // 2
    x_spec = pl.BlockSpec((1, rows, cols), lambda k, xi: (k, 0, 0))
    a_spec = pl.BlockSpec((1, rows, cols), lambda k, xi: (jnp.minimum(k, 1), 0, 0))
    b_spec = pl.BlockSpec((1, rows, cols), lambda k, xi: (jnp.maximum(k - 2, 0), 0, 0))
    part = pl.BlockSpec((cols, 3 * hid), lambda k, xi: (k, 0))

    def body(xi, xrr, x1r, xar, xbr, x3r, y0r, y1r, yar, ybr, y3r, actr, gr, *refs):
        ybuf = refs[-1]
        k = pl.program_id(0)
        for j, y in ((0, y0r), (1, y1r), (3, y3r)):

            @pl.when(k == j)
            def _():
                ybuf[...] = y[...]

        @pl.when(k == 2)
        def _():
            ybuf[: every // 2] = yar[...]
            ybuf[every // 2 :] = ybr[...]

        x2 = jnp.where(k < 2, xar[0], xbr[0])
        x = jnp.concatenate([xrr[0], x1r[0], x2, x3r[0]], axis=0)
        up = dot(x, gr[...], ((0,), (0,)))
        d = dot(actr[...], ybuf[...], ((0,), (0,)))
        squares = [slice(j * hid, (j + 1) * hid) for j in range(cols // hid)]
        if rest is None:
            refs[0][:, : 2 * hid] = up.astype(BF)
            for c in squares:
                refs[0][c, 2 * hid :] = d[:, c].astype(BF)
        else:
            other, og, ou, od = refs[:4]
            og[...] = (up[:, :hid] + other[:, :hid].astype(F32)).astype(BF)
            ou[...] = (up[:, hid:] + other[:, hid : 2 * hid].astype(F32)).astype(BF)
            for c in squares:
                od[:, c] = (d[:, c] + other[c, 2 * hid :].astype(F32)).astype(BF)

    up = pl.BlockSpec((cols, hid), lambda k, xi: ((xi[0] + k) % 4, 0))
    down = pl.BlockSpec((hid, cols), lambda k, xi: (0, (xi[0] + k) % 4))
    return call(
        body,
        (4,),
        [x_spec, x_spec, a_spec, b_spec, x_spec]
        + [same(y.shape) for y in ys]
        + [
            pl.BlockSpec((every, hid), lambda k, xi: (0, which), pipeline_mode=pl.Buffered(1)),
            pl.BlockSpec((every, 2 * hid), lambda k, xi: (0, which), pipeline_mode=pl.Buffered(1)),
        ]
        + ([] if rest is None else [part]),
        part if rest is None else [up, up, down],
        jax.ShapeDtypeStruct((width, 3 * hid), BF)
        if rest is None
        else [
            jax.ShapeDtypeStruct((width, hid), BF),
            jax.ShapeDtypeStruct((width, hid), BF),
            jax.ShapeDtypeStruct((hid, width), BF),
        ],
        (xi, *xs, *ys, act, g) + (() if rest is None else (rest,)),
        2 * 3 * every * width * hid,
        22,
        [pltpu.VMEM((every, cols), BF)],
    )


def add(*parts):
    out = parts[0].astype(F32)
    for p in parts[1:]:
        out = out + p.astype(F32)
    return out.astype(BF)


def tie(values, *late):
    out = lax.optimization_barrier((tuple(values), tuple(late)))
    return out[0]


def shards(tokens, grad_out, gate_prob, expert_ids, w_gate, w_up, w_down):
    rows, width = tokens.shape
    experts = lax.axis_size("expert")
    nx = lax.axis_size("x")
    capacity = rows * 9 // (4 * experts)
    cols = width // nx
    slots = (capacity + 7) // 8 * 8
    half = experts * capacity // 2
    xi = lax.axis_index("x")
    core = lax.axis_index("core")
    on0 = core == 0
    at = jnp.stack([xi, core]).astype(jnp.int32)
    own = (w_gate[0], w_up[0], w_down[0])
    theirs = [swap(w) for w in own]

    sent, pick = dispatch(at, expert_ids.T, gate_prob.T, tokens, grad_out, slots, cols)
    sent = sent.reshape(experts, slots, cols)
    got = lax.all_to_all(sent, "expert", split_axis=0, concat_axis=0, tiled=True)
    got, on0 = tie((got, on0), *theirs)
    got = compact(at, got.reshape(experts * slots, cols), experts, capacity)
    w, wd = pack(at, own, theirs)

    p0 = jnp.stack([got, ring(got, False, -1), ring(got, False, 2), ring(got, False, 1)])

    def sort(kept, come):
        return jnp.where(on0, kept, come), jnp.where(on0, come, kept)

    def flat(y):
        return y.reshape(-1, cols)

    stay = jnp.where(on0, p0[:, :half], p0[:, half:])
    leave = jnp.where(on0, p0[:, half:], p0[:, :half])
    s1, c1 = ring(stay, True, -1), ring(leave, True, -1, cross=True)
    s3, c3 = ring(stay, True, 1), ring(leave, True, 1, cross=True)
    x0, y0 = sort(stay, swap(leave))
    hu0 = hidden_part(at, (x0,), w)
    ga0 = down_part(at, (flat(y0),), (0,), wd)
    s1, c1, s3, c3 = tie((s1, c1, s3, c3), hu0, ga0)
    x1, y1 = sort(s1, c1)
    x3, y3 = sort(s3, c3)
    x2a, x2b = turn(x1[:2], "dp", -1), turn(x3[2:], "dp", 1)
    y2a, y2b = turn(y1[:2], "x", -1), turn(y3[2:], "x", 1)
    hu13 = hidden_part(at, (x1, x3), w)
    ga = down_part(at, (flat(y1), flat(y3)), (1, 3), wd, ga0)
    x2a, x2b, y2a, y2b = tie((x2a, x2b, y2a, y2b), hu13, ga)
    y_all = [flat(y) for y in (y0, y1, y2a, y2b, y3)]
    x_all = (x0, x1, x2a, x2b, x3)
    act, g, keep, send = token_part(at, hu0, hu13, ga, x2a, x2b, y_all[2], y_all[3], w, wd)

    k_up, k_dn = ring(keep[2], False, 1), ring(keep[3], False, -1)
    come = swap(send)
    v_dn, v_up = ring(come[2], False, -1), ring(come[1], False, 1)
    part = weight_part(at, x_all, y_all, act, g, 1)
    k_up, k_dn, v_up, v_dn, part = tie((k_up, k_dn, v_up, v_dn, part))
    k_up = ring(add(keep[1], k_up), False, 1)
    v_dn = ring(add(come[3], v_dn), False, -1)
    part = swap(part)
    total = jnp.stack([add(keep[0], k_up, k_dn), add(come[0], v_up, v_dn)], axis=1)
    parts = [ring(total[k], True, k) for k in (1, 2, 3)]
    gw_gate, gw_up, gw_down = weight_part(at, x_all, y_all, act, g, 0, part)
    parts = tie(parts, gw_gate)
    back = spread(at, [total[0], *parts], experts, slots)

    back = back.reshape(experts, slots, cols // 2)
    back = lax.all_to_all(back, "expert", split_axis=0, concat_axis=0, tiled=True)
    back = back.reshape(experts * slots, cols // 2)
    grad_tokens = dot(pick, back, ((0,), (0,))).astype(BF)
    return grad_tokens, gw_gate[None], gw_up[None], gw_down[None]


def solution(mesh):
    sizes = mesh.devices.shape
    fine = Mesh(
        mesh.devices.reshape(sizes[0], sizes[1], sizes[2] // 2, 2), ("dp", "expert", "x", "core")
    )
    by_token = P(("dp", "expert"), None)
    up = P("expert", None, ("dp", "x", "core"))
    down = P("expert", ("dp", "x", "core"), None)
    return jax.shard_map(
        shards,
        mesh=fine,
        in_specs=(by_token, by_token, by_token, by_token, up, up, down),
        out_specs=(P(("dp", "expert"), ("x", "core")), up, up, down),
        check_vma=False,
    )
```

```python
import jax
import jax.numpy as jnp
from jax import lax
from jax.experimental import pallas as pl
from jax.experimental.pallas import tpu as pltpu
from jax.sharding import Mesh, PartitionSpec as P

BF = jnp.bfloat16
F32 = jnp.float32
INSIDE = pl.BlockSpec(memory_space=pltpu.VMEM)
SCALARS = pl.BlockSpec(memory_space=pltpu.SMEM)


def swap(a):
    return lax.ppermute(a, "core", [(0, 1), (1, 0)])


def ring(a, second, step):
    nd, nx = lax.axis_size("dp"), lax.axis_size("x")
    pairs = []
    for d in range(nd):
        for x in range(nx):
            for c in range(2):
                along_x = (c == 0) != second
                to_d, to_x = (d, (x + step) % nx) if along_x else ((d + step) % nd, x)
                pairs.append(((d * nx + x) * 2 + c, (to_d * nx + to_x) * 2 + c))
    return lax.ppermute(a, ("dp", "x", "core"), pairs)


def dot(a, b, dims):
    return lax.dot_general(a, b, (dims, ((), ())), preferred_element_type=F32)


def add(*parts):
    out = parts[0].astype(F32)
    for p in parts[1:]:
        out = out + p.astype(F32)
    return out.astype(BF)


def tie(values, *late):
    out = lax.optimization_barrier((tuple(values), tuple(late)))
    return out[0]


def same(shape):
    return pl.BlockSpec(shape, lambda k, xi: (0,) * len(shape), pipeline_mode=pl.Buffered(1))


def call(body, grid, in_specs, out_specs, out_shape, args, flops, mib):
    return pl.pallas_call(
        body,
        grid_spec=pltpu.PrefetchScalarGridSpec(
            num_scalar_prefetch=1, grid=grid, in_specs=in_specs, out_specs=out_specs
        ),
        out_shape=out_shape,
        compiler_params=pltpu.CompilerParams(
            dimension_semantics=("arbitrary",), vmem_limit_bytes=mib << 20
        ),
        cost_estimate=pl.CostEstimate(flops=int(flops), bytes_accessed=8 << 20, transcendentals=0),
    )(*args)


def call_inside(body, out_specs, out_shape, args, flops, mib, scratch=()):
    return pl.pallas_call(
        body,
        in_specs=[SCALARS] + [INSIDE] * (len(args) - 1),
        out_specs=out_specs,
        out_shape=out_shape,
        scratch_shapes=scratch,
        compiler_params=pltpu.CompilerParams(vmem_limit_bytes=mib << 20),
        cost_estimate=pl.CostEstimate(flops=int(flops), bytes_accessed=8 << 20, transcendentals=0),
    )(*args)


def x_of(xi):
    return xi[0] // 2


def core_of(xi):
    return xi[0] % 2


def group_of(r, groups, size):
    g = jnp.zeros_like(r)
    for m in range(1, groups):
        g += (r >= m * size).astype(jnp.int32)
    return g


def dispatch(at, ids, gates, tokens, grad_out, half, slots, cols):
    experts = lax.axis_size("expert")
    every, rows = experts * slots, tokens.shape[0]

    def body(xi, ids, gates, tok, grad, sent, pick):
        j = lax.broadcasted_iota(jnp.int32, (every, 1), 0)
        e = group_of(j, experts, slots)
        j = j - e * slots
        is_x, is_y = j < half, (j >= half) & (j < 2 * half)
        s = jnp.where(is_x, j, j - half) + core_of(xi) * half
        first, second = ids[0:1, :] == e, ids[1:2, :] == e
        member = jnp.where(first | second, 1.0, 0.0)
        early = lax.broadcasted_iota(jnp.int32, (rows, rows), 0)
        late = lax.broadcasted_iota(jnp.int32, (rows, rows), 1)
        before = jnp.where(early < late, 1.0, 0.0).astype(BF)
        slot = dot(member.astype(BF), before, ((1,), (0,)))
        hit = jnp.where(slot == s.astype(F32), member, 0.0)
        hit_x, hit_y = jnp.where(is_x, hit, 0.0), jnp.where(is_y, hit, 0.0)
        gate = jnp.where(first, gates[0:1, :], 0.0) + jnp.where(second, gates[1:2, :], 0.0)
        gate = jnp.sum(hit_y * gate, axis=1, keepdims=True)
        x = dot(hit_x.astype(BF), tok[...], ((1,), (0,)))
        y = dot(hit_y.astype(BF), grad[...], ((1,), (0,))) * gate
        sent[...] = (x + y).astype(BF)
        pick[...] = (hit_x + hit_y).astype(BF)

    column = pl.BlockSpec((rows, cols), lambda k, xi: (0, x_of(xi)))
    return call(
        body,
        (1,),
        [same(ids.shape), same(gates.shape), column, column],
        [same((every, cols)), same((every, rows))],
        [jax.ShapeDtypeStruct((every, cols), BF), jax.ShapeDtypeStruct((every, rows), BF)],
        (at, ids, gates, tokens, grad_out),
        4 * every * rows * cols,
        56,
    )


def compact(at, got, experts, half):
    rows, cols = got.shape
    slots = rows // experts
    side = experts * half

    def body(xi, a, out):
        r = lax.broadcasted_iota(jnp.int32, (2 * side, 1), 0)
        is_y = (r >= side).astype(jnp.int32)
        r = r - is_y * side
        e = group_of(r, experts, half)
        place = e * slots + is_y * half + r - e * half
        q = lax.broadcasted_iota(jnp.int32, (2 * side, rows), 1)
        m = jnp.where(q == place, 1.0, 0.0).astype(BF)
        out[...] = dot(m, a[...], ((1,), (0,))).astype(BF)

    return call_inside(
        body,
        INSIDE,
        jax.ShapeDtypeStruct((2 * side, cols), BF),
        (at, got),
        4 * side * rows * cols,
        8,
    )


def spread(at, parts, experts, slots):
    side, cols = parts[0].shape
    half = side // experts
    rows = experts * slots

    def body(xi, *refs):
        *ins, out = refs
        total = ins[0][...].astype(F32)
        for a in ins[1:]:
            total += a[...].astype(F32)
        total = total.astype(BF)
        j = lax.broadcasted_iota(jnp.int32, (rows, 1), 0)
        e = group_of(j, experts, slots)
        j = j - e * slots
        q = lax.broadcasted_iota(jnp.int32, (rows, side), 1)
        low = jnp.where((q == e * half + j) & (j < half), 1.0, 0.0).astype(BF)
        high = (q == e * half + j - half) & (j >= half) & (j < 2 * half)
        high = jnp.where(high, 1.0, 0.0).astype(BF)
        out[...] = (
            dot(low, total[:, : cols // 2], ((1,), (0,)))
            + dot(high, total[:, cols // 2 :], ((1,), (0,)))
        ).astype(BF)

    return call_inside(
        body,
        INSIDE,
        jax.ShapeDtypeStruct((rows, cols // 2), BF),
        (at, *parts),
        2 * rows * side * cols,
        8,
    )


def combine(at, pick, back, experts, half):
    rows, tokens = pick.shape
    cols = back.shape[1]
    slots = rows // experts

    def body(xi, pick, back, mine, other):
        j = lax.broadcasted_iota(jnp.int32, (rows, 1), 0)
        j = j - group_of(j, experts, slots) * slots
        a = back[...]
        none = jnp.zeros_like(a)
        low = dot(pick[...], jnp.where(j < half, a, none), ((0,), (0,)))
        high = dot(pick[...], jnp.where(j >= half, a, none), ((0,), (0,)))
        on0 = core_of(xi) == 0
        mine[...] = jnp.where(on0, low, high)
        other[...] = jnp.where(on0, high, low)

    shape = jax.ShapeDtypeStruct((tokens, cols), F32)
    return call_inside(
        body, [INSIDE] * 2, [shape] * 2, (at, pick, back), 4 * rows * tokens * cols, 8
    )


def pack(at, own, theirs):
    width, hid = own[0].shape
    cols = width // 4
    up = pl.BlockSpec((cols, hid), lambda k, xi: ((x_of(xi) + k) % 4, 0))
    down = pl.BlockSpec((hid, cols), lambda k, xi: (0, (x_of(xi) + k) % 4))

    def body(xi, g1, u1, d1, g2, u2, d2, w, wd):
        for j, ref in enumerate((g1, u1, g2, u2)):
            w[0, :, j * hid : (j + 1) * hid] = ref[...]
        wd[0, :hid] = d1[...]
        wd[0, hid:] = d2[...]

    return call(
        body,
        (4,),
        [up, up, down] * 2,
        [
            pl.BlockSpec((1, cols, 4 * hid), lambda k, xi: (k, 0, 0)),
            pl.BlockSpec((1, 2 * hid, cols), lambda k, xi: (k, 0, 0)),
        ],
        [
            jax.ShapeDtypeStruct((4, cols, 4 * hid), BF),
            jax.ShapeDtypeStruct((4, 2 * hid, cols), BF),
        ],
        (at, *own, *theirs),
        width * hid,
        14,
    )


def put_in(xi, hu, ga, piece, first, s, w, wd):
    on0 = core_of(xi) == 0
    row, col = jnp.where(on0, s, first), jnp.where(on0, first, s)
    rows = hu.shape[1]
    hu[row] += dot(piece[:rows], w[col], ((1,), (0,)))
    ga[row] += dot(piece[rows:], wd[col], ((1,), (1,)))


def early_part(at, pieces, places, w, wd, so_far=None):
    n = len(pieces)
    rows = pieces[0].shape[1] // 2
    count = pieces[0].shape[0]
    more = [] if so_far is None else list(so_far)

    def body(xi, *refs):
        ps, w, wd, hu, ga = refs[:n], refs[n], refs[n + 1], refs[-2], refs[-1]
        if more:
            hu[...] = refs[n + 2][...]
            ga[...] = refs[n + 3][...]
        else:
            hu[...] = jnp.zeros_like(hu)
            ga[...] = jnp.zeros_like(ga)

        @pl.loop(0, count)
        def _(k):
            for p, (first, s) in zip(ps, places):
                put_in(xi, hu, ga, p.at[k], first + k, s, w, wd)

    shapes = [
        jax.ShapeDtypeStruct((4, rows, w.shape[2]), F32),
        jax.ShapeDtypeStruct((4, rows, wd.shape[1]), F32),
    ]
    return call_inside(
        body,
        [INSIDE] * 2,
        shapes,
        (at, *pieces, w, wd, *more),
        2 * n * count * rows * w.shape[1] * (w.shape[2] + wd.shape[1]),
        12,
    )


def token_part(at, hu, ga, p2a, p2b, w, wd):
    rows = hu.shape[1]
    cols = w.shape[1]
    hid = w.shape[2] // 4
    every = 4 * rows

    def body(xi, hu, ga, pa, pb, w, wd, act, g, keep):
        def finish(k, hu2, ga2):
            r = slice(k * rows, (k + 1) * rows)
            for c in range(2):
                part = slice(c * hid, (c + 1) * hid)
                hs = slice(2 * c * hid, (2 * c + 1) * hid)
                us = slice((2 * c + 1) * hid, (2 * c + 2) * hid)
                hh, uu, gg = hu[k, :, hs], hu[k, :, us], ga[k, :, part]
                if hu2 is not None:
                    hh, uu, gg = hh + hu2[:, hs], uu + hu2[:, us], gg + ga2[:, part]
                s = jax.nn.sigmoid(hh)
                silu = hh * s
                act[r, part] = (silu * uu).astype(BF)
                g[r, hs] = (gg * uu * (s * (1.0 + hh * (1.0 - s)))).astype(BF)
                g[r, us] = (gg * silu).astype(BF)

        last = ((pa, 0), (pa, 1), (pb, 0), (pb, 1))

        @pl.when(core_of(xi) == 0)
        def _():
            hu2 = ga2 = 0.0
            for k, (p, n) in enumerate(last):
                hu2 += dot(p[n, :rows], w[k], ((1,), (0,)))
                ga2 += dot(p[n, rows:], wd[k], ((1,), (1,)))
            for k in range(4):
                finish(k, *((hu2, ga2) if k == 2 else (None, None)))

        @pl.when(core_of(xi) == 1)
        def _():
            for k, (p, n) in enumerate(last):
                hu2 = dot(p[n, :rows], w[2], ((1,), (0,)))
                finish(k, hu2, dot(p[n, rows:], wd[2], ((1,), (1,))))

        @pl.loop(0, 4)
        def _(k):
            out = dot(g[...], w[k], ((1,), (1,))).astype(BF)

            @pl.when(core_of(xi) == 0)
            def _():
                for j in range(4):
                    keep[k, j] = out[j * rows : (j + 1) * rows]

            @pl.when(core_of(xi) == 1)
            def _():
                for j in range(4):
                    keep[j, k] = out[j * rows : (j + 1) * rows]

    return call_inside(
        body,
        [INSIDE] * 3,
        [
            jax.ShapeDtypeStruct((every, 2 * hid), BF),
            jax.ShapeDtypeStruct((every, 4 * hid), BF),
            jax.ShapeDtypeStruct((4, 4, rows, cols), BF),
        ],
        (at, hu, ga, p2a, p2b, w, wd),
        2 * every * 4 * cols * 4 * hid,
        20,
    )


def weight_part(at, pieces, act, g, which, dtype):
    p0 = pieces[0]
    rows, cols = p0.shape[1] // 2, p0.shape[2]
    every, width = 4 * rows, 4 * cols
    hid = act.shape[1] // 2
    squares = [slice(j * hid, (j + 1) * hid) for j in range(cols // hid)]

    def body(xi, p0, p1a, p1b, p2a, p2b, p3a, p3b, act, g, *refs):
        xbuf, ybuf = refs[-2:]

        def load(sources):
            for j, (ref, n) in enumerate(sources):
                xbuf[j * rows : (j + 1) * rows] = ref[n, :rows]
                ybuf[j * rows : (j + 1) * rows] = ref[n, rows:]

        def step(k):
            on0 = core_of(xi) == 0

            @pl.when(on0 & (k < 2))
            def _():
                load([(p0, k), (p1a, k), (p2a, k), (p3a, k)])

            @pl.when(on0 & (k >= 2))
            def _():
                load([(p0, k), (p1b, k - 2), (p2b, k - 2), (p3b, k - 2)])

            for n, (a, b) in enumerate(((p0, p0), (p1a, p1b), (p2a, p2b), (p3a, p3b))):

                @pl.when(jnp.logical_not(on0) & (k == n))
                def _():
                    shift = 2 if a is b else 0
                    load([(a, 0), (a, 1), (b, shift), (b, shift + 1)])

            cut = slice(which * hid, (which + 1) * hid)
            cut2 = slice(2 * which * hid, 2 * (which + 1) * hid)
            return (
                dot(xbuf[...], g[:, cut2], ((0,), (0,))),
                dot(act[:, cut], ybuf[...], ((0,), (0,))),
            )

        out = refs[0]

        @pl.loop(0, 4)
        def _(k):
            up, down = step(k)
            out[k, :, : 2 * hid] = up.astype(out.dtype)
            for c in squares:
                out[k, c, 2 * hid :] = down[:, c].astype(out.dtype)

    return call_inside(
        body,
        INSIDE,
        jax.ShapeDtypeStruct((4, cols, 3 * hid), dtype),
        (at, *pieces, act, g),
        2 * 3 * every * width * hid,
        14,
        [pltpu.VMEM((every, cols), BF)] * 2,
    )


def weight_sum(at, mine, other):
    _, cols, hid = mine.shape
    hid //= 3
    width = 4 * cols

    def body(xi, mine, other, og, ou, od, sg, su, sd, sems):
        def copies(k):
            block = pl.ds(pl.multiple_of((x_of(xi) + k) % 4 * cols, cols), cols)
            return (
                pltpu.make_async_copy(sg.at[k], og.at[block, :], sems.at[k, 0]),
                pltpu.make_async_copy(su.at[k], ou.at[block, :], sems.at[k, 1]),
                pltpu.make_async_copy(sd.at[k], od.at[:, block], sems.at[k, 2]),
            )

        @pl.loop(0, 4)
        def _(k):
            total = (mine[k] + other[k].astype(F32)).astype(BF)
            sg[k] = total[:, :hid]
            su[k] = total[:, hid : 2 * hid]
            for j in range(cols // hid):
                c = slice(j * hid, (j + 1) * hid)
                sd[k, :, c] = total[c, 2 * hid :]
            for copy in copies(k):
                copy.start()

        @pl.loop(0, 4)
        def _(k):
            for copy in copies(k):
                copy.wait()

    return call_inside(
        body,
        [pl.BlockSpec(memory_space=pl.ANY)] * 3,
        [
            jax.ShapeDtypeStruct((width, hid), BF),
            jax.ShapeDtypeStruct((width, hid), BF),
            jax.ShapeDtypeStruct((hid, width), BF),
        ],
        (at, mine, other),
        12 * width * hid,
        14,
        [
            pltpu.VMEM((4, cols, hid), BF),
            pltpu.VMEM((4, cols, hid), BF),
            pltpu.VMEM((4, hid, cols), BF),
            pltpu.SemaphoreType.DMA((4, 3)),
        ],
    )


def shards(tokens, grad_out, gate_prob, expert_ids, w_gate, w_up, w_down):
    rows, width = tokens.shape
    experts = lax.axis_size("expert")
    capacity = rows * 9 // (4 * experts)
    half = capacity // 2
    cols = width // lax.axis_size("x")
    slots = (capacity + 7) // 8 * 8
    at = lax.axis_index(("x", "core")).astype(jnp.int32).reshape(1)
    own = (w_gate[0], w_up[0], w_down[0])
    theirs = [swap(w) for w in own]

    def exchange(a):
        a = a.reshape(experts, slots, -1)
        a = lax.all_to_all(a, "expert", split_axis=0, concat_axis=0, tiled=True)
        return a.reshape(experts * slots, -1)

    sent, pick = dispatch(at, expert_ids.T, gate_prob.T, tokens, grad_out, half, slots, cols)
    (got,) = tie((exchange(sent),), *theirs)
    got = compact(at, got, experts, half)
    w, wd = pack(at, own, theirs)

    p0 = jnp.stack([got, ring(got, False, -1), ring(got, False, 2), ring(got, False, 1)])
    p1a, p3b = ring(p0[:2], True, -1), ring(p0[2:], True, 1)
    p1b, p3a = ring(p0[2:], True, -1), ring(p0[:2], True, 1)
    early = early_part(at, (p0,), ((0, 0),), w, wd)
    p1a, p3b = tie((p1a, p3b), *early)
    p2a, p2b = ring(p1a, True, -1), ring(p3b, True, 1)
    places = ((0, 1), (2, 1), (0, 3), (2, 3))
    hu, ga = early_part(at, (p1a, p1b, p3a, p3b), places, w, wd, early)
    p2a, p2b = tie((p2a, p2b), hu, ga)
    act, g, keep = token_part(at, hu, ga, p2a, p2b, w, wd)
    pieces = (p0, p1a, p1b, p2a, p2b, p3a, p3b)

    k_up, v_dn = ring(keep[2, :2], False, 1), ring(keep[2, 2:], False, -1)
    part = weight_part(at, pieces, act, g, 1, BF)
    k_up, v_dn, part, keep = tie((k_up, v_dn, part, keep))
    k_up, v_dn = tie((add(keep[1, :2], k_up), add(keep[3, 2:], v_dn)))
    k_up, v_dn = ring(k_up, False, 1), ring(v_dn, False, -1)
    v_up, k_dn = ring(keep[1, 2:], False, 1), ring(keep[3, :2], False, -1)
    part = swap(part)
    mine = weight_part(at, pieces, act, g, 0, F32)
    k_up, v_dn, v_up, k_dn = tie((k_up, v_dn, v_up, k_dn), mine)
    total = jnp.concatenate([add(keep[0, :2], k_up, k_dn), add(keep[0, 2:], v_up, v_dn)], axis=0)
    parts = [ring(total[k], True, k) for k in (1, 2, 3)]
    gw_gate, gw_up, gw_down = weight_sum(at, mine, part)
    parts = tie(parts, gw_gate)

    back = exchange(spread(at, [total[0], *parts], experts, slots))
    mine, other = combine(at, pick, back, experts, half)
    grad_tokens = (mine + swap(other)).astype(BF)
    return grad_tokens, gw_gate[None], gw_up[None], gw_down[None]


def solution(mesh):
    sizes = mesh.devices.shape
    fine = Mesh(
        mesh.devices.reshape(sizes[0], sizes[1], sizes[2] // 2, 2), ("dp", "expert", "x", "core")
    )
    by_token = P(("dp", "expert"), None)
    up = P("expert", None, ("dp", "x", "core"))
    down = P("expert", ("dp", "x", "core"), None)
    return jax.shard_map(
        shards,
        mesh=fine,
        in_specs=(by_token, by_token, by_token, by_token, up, up, down),
        out_specs=(P(("dp", "expert"), ("x", "core")), up, up, down),
        check_vma=False,
    )
```

```python
import jax
import jax.numpy as jnp
from jax import lax
from jax.experimental import pallas as pl
from jax.experimental.pallas import tpu as pltpu
from jax.sharding import Mesh, PartitionSpec as P

BF = jnp.bfloat16
F32 = jnp.float32
INSIDE = pl.BlockSpec(memory_space=pltpu.VMEM)
SCALARS = pl.BlockSpec(memory_space=pltpu.SMEM)


def swap(a):
    return lax.ppermute(a, "core", [(0, 1), (1, 0)])


def ring(a, second, step):
    nd, nx = lax.axis_size("dp"), lax.axis_size("x")
    pairs = []
    for d in range(nd):
        for x in range(nx):
            for c in range(2):
                along_x = (c == 0) != second
                to_d, to_x = (d, (x + step) % nx) if along_x else ((d + step) % nd, x)
                pairs.append(((d * nx + x) * 2 + c, (to_d * nx + to_x) * 2 + c))
    return lax.ppermute(a, ("dp", "x", "core"), pairs)


def dot(a, b, dims):
    return lax.dot_general(a, b, (dims, ((), ())), preferred_element_type=F32)


def add(*parts):
    out = parts[0].astype(F32)
    for p in parts[1:]:
        out = out + p.astype(F32)
    return out.astype(BF)


def tie(values, *late):
    out = lax.optimization_barrier((tuple(values), tuple(late)))
    return out[0]


def same(shape):
    return pl.BlockSpec(shape, lambda k, xi: (0,) * len(shape), pipeline_mode=pl.Buffered(1))


def call(body, grid, in_specs, out_specs, out_shape, args, flops, mib):
    return pl.pallas_call(
        body,
        grid_spec=pltpu.PrefetchScalarGridSpec(
            num_scalar_prefetch=1, grid=grid, in_specs=in_specs, out_specs=out_specs
        ),
        out_shape=out_shape,
        compiler_params=pltpu.CompilerParams(
            dimension_semantics=("arbitrary",), vmem_limit_bytes=mib << 20
        ),
        cost_estimate=pl.CostEstimate(flops=int(flops), bytes_accessed=8 << 20, transcendentals=0),
    )(*args)


def call_inside(body, out_specs, out_shape, args, flops, mib, scratch=()):
    return pl.pallas_call(
        body,
        in_specs=[SCALARS] + [INSIDE] * (len(args) - 1),
        out_specs=out_specs,
        out_shape=out_shape,
        scratch_shapes=scratch,
        compiler_params=pltpu.CompilerParams(vmem_limit_bytes=mib << 20),
        cost_estimate=pl.CostEstimate(flops=int(flops), bytes_accessed=8 << 20, transcendentals=0),
    )(*args)


def x_of(xi):
    return xi[0] // 2


def core_of(xi):
    return xi[0] % 2


def group_of(r, groups, size):
    g = jnp.zeros_like(r)
    for m in range(1, groups):
        g += (r >= m * size).astype(jnp.int32)
    return g


def dispatch(at, ids, gates, tokens, grad_out, half, slots, cols):
    experts = lax.axis_size("expert")
    every, rows = experts * slots, tokens.shape[0]

    def body(xi, ids, gates, tok, grad, sent, pick):
        j = lax.broadcasted_iota(jnp.int32, (every, 1), 0)
        e = group_of(j, experts, slots)
        j = j - e * slots
        is_x, is_y = j < half, (j >= half) & (j < 2 * half)
        s = jnp.where(is_x, j, j - half) + core_of(xi) * half
        first, second = ids[0:1, :] == e, ids[1:2, :] == e
        member = jnp.where(first | second, 1.0, 0.0)
        early = lax.broadcasted_iota(jnp.int32, (rows, rows), 0)
        late = lax.broadcasted_iota(jnp.int32, (rows, rows), 1)
        before = jnp.where(early < late, 1.0, 0.0).astype(BF)
        slot = dot(member.astype(BF), before, ((1,), (0,)))
        hit = jnp.where(slot == s.astype(F32), member, 0.0)
        hit_x, hit_y = jnp.where(is_x, hit, 0.0), jnp.where(is_y, hit, 0.0)
        gate = jnp.where(first, gates[0:1, :], 0.0) + jnp.where(second, gates[1:2, :], 0.0)
        gate = jnp.sum(hit_y * gate, axis=1, keepdims=True)
        x = dot(hit_x.astype(BF), tok[...], ((1,), (0,)))
        y = dot(hit_y.astype(BF), grad[...], ((1,), (0,))) * gate
        sent[...] = (x + y).astype(BF)
        pick[...] = (hit_x + hit_y).astype(BF)

    column = pl.BlockSpec((rows, cols), lambda k, xi: (0, x_of(xi)))
    return call(
        body,
        (1,),
        [same(ids.shape), same(gates.shape), column, column],
        [same((every, cols)), same((every, rows))],
        [jax.ShapeDtypeStruct((every, cols), BF), jax.ShapeDtypeStruct((every, rows), BF)],
        (at, ids, gates, tokens, grad_out),
        4 * every * rows * cols,
        56,
    )


def compact(at, got, experts, half):
    rows, cols = got.shape
    slots = rows // experts
    side = experts * half

    def body(xi, a, out):
        r = lax.broadcasted_iota(jnp.int32, (2 * side, 1), 0)
        is_y = (r >= side).astype(jnp.int32)
        r = r - is_y * side
        e = group_of(r, experts, half)
        place = e * slots + is_y * half + r - e * half
        q = lax.broadcasted_iota(jnp.int32, (2 * side, rows), 1)
        m = jnp.where(q == place, 1.0, 0.0).astype(BF)
        out[...] = dot(m, a[...], ((1,), (0,))).astype(BF)

    return call_inside(
        body,
        INSIDE,
        jax.ShapeDtypeStruct((2 * side, cols), BF),
        (at, got),
        4 * side * rows * cols,
        8,
    )


def spread(at, parts, experts, slots):
    side, cols = parts[0].shape
    half = side // experts
    rows = experts * slots

    def body(xi, *refs):
        *ins, out = refs
        total = ins[0][...].astype(F32)
        for a in ins[1:]:
            total += a[...].astype(F32)
        total = total.astype(BF)
        j = lax.broadcasted_iota(jnp.int32, (rows, 1), 0)
        e = group_of(j, experts, slots)
        j = j - e * slots
        q = lax.broadcasted_iota(jnp.int32, (rows, side), 1)
        low = jnp.where((q == e * half + j) & (j < half), 1.0, 0.0).astype(BF)
        high = (q == e * half + j - half) & (j >= half) & (j < 2 * half)
        high = jnp.where(high, 1.0, 0.0).astype(BF)
        out[...] = (
            dot(low, total[:, : cols // 2], ((1,), (0,)))
            + dot(high, total[:, cols // 2 :], ((1,), (0,)))
        ).astype(BF)

    return call_inside(
        body,
        INSIDE,
        jax.ShapeDtypeStruct((rows, cols // 2), BF),
        (at, *parts),
        2 * rows * side * cols,
        8,
    )


def combine(at, pick, back, experts, half):
    rows, tokens = pick.shape
    cols = back.shape[1]
    slots = rows // experts

    def body(xi, pick, back, mine, other):
        j = lax.broadcasted_iota(jnp.int32, (rows, 1), 0)
        j = j - group_of(j, experts, slots) * slots
        a = back[...]
        none = jnp.zeros_like(a)
        low = dot(pick[...], jnp.where(j < half, a, none), ((0,), (0,)))
        high = dot(pick[...], jnp.where(j >= half, a, none), ((0,), (0,)))
        on0 = core_of(xi) == 0
        mine[...] = jnp.where(on0, low, high)
        other[...] = jnp.where(on0, high, low)

    shape = jax.ShapeDtypeStruct((tokens, cols), F32)
    return call_inside(
        body, [INSIDE] * 2, [shape] * 2, (at, pick, back), 4 * rows * tokens * cols, 8
    )


def pack(at, own, theirs):
    width, hid = own[0].shape
    cols = width // 4
    up = pl.BlockSpec((cols, hid), lambda k, xi: ((x_of(xi) + k) % 4, 0))
    down = pl.BlockSpec((hid, cols), lambda k, xi: (0, (x_of(xi) + k) % 4))

    def body(xi, g1, u1, d1, g2, u2, d2, w, wd):
        for j, ref in enumerate((g1, u1, g2, u2)):
            w[0, :, j * hid : (j + 1) * hid] = ref[...]
        wd[0, :hid] = d1[...]
        wd[0, hid:] = d2[...]

    return call(
        body,
        (4,),
        [up, up, down] * 2,
        [
            pl.BlockSpec((1, cols, 4 * hid), lambda k, xi: (k, 0, 0)),
            pl.BlockSpec((1, 2 * hid, cols), lambda k, xi: (k, 0, 0)),
        ],
        [
            jax.ShapeDtypeStruct((4, cols, 4 * hid), BF),
            jax.ShapeDtypeStruct((4, 2 * hid, cols), BF),
        ],
        (at, *own, *theirs),
        width * hid,
        14,
    )


def put_in(xi, hu, ga, piece, first, s, w, wd):
    on0 = core_of(xi) == 0
    row, col = jnp.where(on0, s, first), jnp.where(on0, first, s)
    rows = hu.shape[1]
    hu[row] += dot(piece[:rows], w[col], ((1,), (0,)))
    ga[row] += dot(piece[rows:], wd[col], ((1,), (1,)))


def early_part(at, pieces, places, w, wd, so_far=None):
    n = len(pieces)
    rows = pieces[0].shape[1] // 2
    count = pieces[0].shape[0]
    more = [] if so_far is None else list(so_far)

    def body(xi, *refs):
        ps, w, wd, hu, ga = refs[:n], refs[n], refs[n + 1], refs[-2], refs[-1]
        if more:
            hu[...] = refs[n + 2][...]
            ga[...] = refs[n + 3][...]
        else:
            hu[...] = jnp.zeros_like(hu)
            ga[...] = jnp.zeros_like(ga)

        @pl.loop(0, count)
        def _(k):
            for p, (first, s) in zip(ps, places):
                put_in(xi, hu, ga, p.at[k], first + k, s, w, wd)

    shapes = [
        jax.ShapeDtypeStruct((4, rows, w.shape[2]), F32),
        jax.ShapeDtypeStruct((4, rows, wd.shape[1]), F32),
    ]
    return call_inside(
        body,
        [INSIDE] * 2,
        shapes,
        (at, *pieces, w, wd, *more),
        2 * n * count * rows * w.shape[1] * (w.shape[2] + wd.shape[1]),
        12,
    )


def token_part(at, hu, ga, p2a, p2b, w, wd):
    rows = hu.shape[1]
    cols = w.shape[1]
    hid = w.shape[2] // 4
    every = 4 * rows

    def body(xi, hu, ga, pa, pb, w, wd, act, g, keep):
        def finish(k, hu2, ga2):
            r = slice(k * rows, (k + 1) * rows)
            for c in range(2):
                part = slice(c * hid, (c + 1) * hid)
                hs = slice(2 * c * hid, (2 * c + 1) * hid)
                us = slice((2 * c + 1) * hid, (2 * c + 2) * hid)
                hh, uu, gg = hu[k, :, hs], hu[k, :, us], ga[k, :, part]
                if hu2 is not None:
                    hh, uu, gg = hh + hu2[:, hs], uu + hu2[:, us], gg + ga2[:, part]
                s = jax.nn.sigmoid(hh)
                silu = hh * s
                act[r, part] = (silu * uu).astype(BF)
                g[r, hs] = (gg * uu * (s * (1.0 + hh * (1.0 - s)))).astype(BF)
                g[r, us] = (gg * silu).astype(BF)

        last = ((pa, 0), (pa, 1), (pb, 0), (pb, 1))

        @pl.when(core_of(xi) == 0)
        def _():
            hu2 = ga2 = 0.0
            for k, (p, n) in enumerate(last):
                hu2 += dot(p[n, :rows], w[k], ((1,), (0,)))
                ga2 += dot(p[n, rows:], wd[k], ((1,), (1,)))
            for k in range(4):
                finish(k, *((hu2, ga2) if k == 2 else (None, None)))

        @pl.when(core_of(xi) == 1)
        def _():
            x = jnp.concatenate([p[n, :rows] for p, n in last], axis=0)
            y = jnp.concatenate([p[n, rows:] for p, n in last], axis=0)
            hu2 = dot(x, w[2], ((1,), (0,)))
            ga2 = dot(y, wd[2], ((1,), (1,)))
            for k in range(4):
                r = slice(k * rows, (k + 1) * rows)
                finish(k, hu2[r], ga2[r])

        @pl.when(core_of(xi) == 0)
        def _():
            out = dot(g[...], w[2], ((1,), (1,))).astype(BF)
            for j in range(4):
                keep[j] = out[j * rows : (j + 1) * rows]

        @pl.when(core_of(xi) == 1)
        def _():
            mine = g[2 * rows : 3 * rows]
            for k in range(4):
                keep[k] = dot(mine, w[k], ((1,), (1,))).astype(BF)

    return call_inside(
        body,
        [INSIDE] * 3,
        [
            jax.ShapeDtypeStruct((every, 2 * hid), BF),
            jax.ShapeDtypeStruct((every, 4 * hid), BF),
            jax.ShapeDtypeStruct((4, rows, cols), BF),
        ],
        (at, hu, ga, p2a, p2b, w, wd),
        every * 4 * cols * 4 * hid,
        20,
    )


def other_blocks(at, g, w):
    cols = w.shape[1]
    rows = g.shape[0] // 4
    places = (0, 1, 3)

    def body(xi, g, w, keep):
        @pl.when(core_of(xi) == 0)
        def _():
            for n, k in enumerate(places):
                out = dot(g[...], w[k], ((1,), (1,))).astype(BF)
                for j in range(4):
                    keep[n, j] = out[j * rows : (j + 1) * rows]

        @pl.when(core_of(xi) == 1)
        def _():
            mine = jnp.concatenate([g[: 2 * rows], g[3 * rows :]], axis=0)

            @pl.loop(0, 4)
            def _(k):
                out = dot(mine, w[k], ((1,), (1,))).astype(BF)
                for n in range(3):
                    keep[n, k] = out[n * rows : (n + 1) * rows]

    return call_inside(
        body,
        INSIDE,
        jax.ShapeDtypeStruct((3, 4, rows, cols), BF),
        (at, g, w),
        2 * 3 * rows * 4 * cols * w.shape[2],
        12,
    )


def weight_part(at, pieces, act, g, which, dtype, up=True, down=True):
    p0 = pieces[0]
    rows, cols = p0.shape[1] // 2, p0.shape[2]
    every, width = 4 * rows, 4 * cols
    hid = act.shape[1] // 2
    squares = [slice(j * hid, (j + 1) * hid) for j in range(cols // hid)]
    size = (2 * up + down) * hid

    def body(xi, p0, p1a, p1b, p2a, p2b, p3a, p3b, act, g, *refs):
        xbuf, ybuf = refs[-2:]

        def load(sources):
            for j, (ref, n) in enumerate(sources):
                if up:
                    xbuf[j * rows : (j + 1) * rows] = ref[n, :rows]
                if down:
                    ybuf[j * rows : (j + 1) * rows] = ref[n, rows:]

        def step(k):
            on0 = core_of(xi) == 0

            @pl.when(on0 & (k < 2))
            def _():
                load([(p0, k), (p1a, k), (p2a, k), (p3a, k)])

            @pl.when(on0 & (k >= 2))
            def _():
                load([(p0, k), (p1b, k - 2), (p2b, k - 2), (p3b, k - 2)])

            for n, (a, b) in enumerate(((p0, p0), (p1a, p1b), (p2a, p2b), (p3a, p3b))):

                @pl.when(jnp.logical_not(on0) & (k == n))
                def _():
                    shift = 2 if a is b else 0
                    load([(a, 0), (a, 1), (b, shift), (b, shift + 1)])

            cut = slice(which * hid, (which + 1) * hid)
            cut2 = slice(2 * which * hid, 2 * (which + 1) * hid)
            return (
                dot(xbuf[...], g[:, cut2], ((0,), (0,))) if up else None,
                dot(act[:, cut], ybuf[...], ((0,), (0,))) if down else None,
            )

        out = refs[0]

        @pl.loop(0, 4)
        def _(k):
            for_up, for_down = step(k)
            if up:
                out[k, :, : 2 * hid] = for_up.astype(out.dtype)
            if down:
                for c in squares:
                    out[k, c, size - hid :] = for_down[:, c].astype(out.dtype)

    return call_inside(
        body,
        INSIDE,
        jax.ShapeDtypeStruct((4, cols, size), dtype),
        (at, *pieces, act, g),
        2 * every * width * size,
        14,
        [pltpu.VMEM((every, cols), BF)] * 2,
    )


def weight_sum(at, mine, other_up, other_down):
    _, cols, hid = mine.shape
    hid //= 3
    width = 4 * cols

    def body(xi, mine, up, down, og, ou, od, sg, su, sd, sems):
        def copies(k):
            block = pl.ds(pl.multiple_of((x_of(xi) + k) % 4 * cols, cols), cols)
            return (
                pltpu.make_async_copy(sg.at[k], og.at[block, :], sems.at[k, 0]),
                pltpu.make_async_copy(su.at[k], ou.at[block, :], sems.at[k, 1]),
                pltpu.make_async_copy(sd.at[k], od.at[:, block], sems.at[k, 2]),
            )

        @pl.loop(0, 4)
        def _(k):
            total = (mine[k, :, : 2 * hid] + up[k].astype(F32)).astype(BF)
            sg[k] = total[:, :hid]
            su[k] = total[:, hid:]
            total = (mine[k, :, 2 * hid :] + down[k].astype(F32)).astype(BF)
            for j in range(cols // hid):
                c = slice(j * hid, (j + 1) * hid)
                sd[k, :, c] = total[c]
            for copy in copies(k):
                copy.start()

        @pl.loop(0, 4)
        def _(k):
            for copy in copies(k):
                copy.wait()

    return call_inside(
        body,
        [pl.BlockSpec(memory_space=pl.ANY)] * 3,
        [
            jax.ShapeDtypeStruct((width, hid), BF),
            jax.ShapeDtypeStruct((width, hid), BF),
            jax.ShapeDtypeStruct((hid, width), BF),
        ],
        (at, mine, other_up, other_down),
        12 * width * hid,
        14,
        [
            pltpu.VMEM((4, cols, hid), BF),
            pltpu.VMEM((4, cols, hid), BF),
            pltpu.VMEM((4, hid, cols), BF),
            pltpu.SemaphoreType.DMA((4, 3)),
        ],
    )


def shards(tokens, grad_out, gate_prob, expert_ids, w_gate, w_up, w_down):
    rows, width = tokens.shape
    experts = lax.axis_size("expert")
    capacity = rows * 9 // (4 * experts)
    half = capacity // 2
    cols = width // lax.axis_size("x")
    slots = (capacity + 7) // 8 * 8
    at = lax.axis_index(("x", "core")).astype(jnp.int32).reshape(1)
    own = (w_gate[0], w_up[0], w_down[0])
    theirs = [swap(w) for w in own]

    def exchange(a):
        a = a.reshape(experts, slots, -1)
        a = lax.all_to_all(a, "expert", split_axis=0, concat_axis=0, tiled=True)
        return a.reshape(experts * slots, -1)

    sent, pick = dispatch(at, expert_ids.T, gate_prob.T, tokens, grad_out, half, slots, cols)
    (got,) = tie((exchange(sent),), *theirs)
    got = compact(at, got, experts, half)
    w, wd = pack(at, own, theirs)

    f1, f3, f2 = ring(got, False, -1), ring(got, False, 1), ring(got, False, 2)
    p0 = jnp.stack([got, f1, f2, f3])
    p1a, p3b = ring(p0[:2], True, -1), ring(p0[2:], True, 1)
    p1b, p3a = ring(p0[2:], True, -1), ring(p0[:2], True, 1)
    early = early_part(at, (p0,), ((0, 0),), w, wd)
    p1a, p3b = tie((p1a, p3b), *early)
    p2a, p2b = ring(p1a, True, -1), ring(p3b, True, 1)
    places = ((0, 1), (2, 1), (0, 3), (2, 3))
    hu, ga = early_part(at, (p1a, p1b, p3a, p3b), places, w, wd, early)
    p2a, p2b = tie((p2a, p2b), hu, ga)
    act, g, first = token_part(at, hu, ga, p2a, p2b, w, wd)
    pieces = (p0, p1a, p1b, p2a, p2b, p3a, p3b)

    k_up, v_dn = ring(first[:2], False, 1), ring(first[2:], False, -1)
    keep = other_blocks(at, g, w)
    part = weight_part(at, pieces, act, g, 1, BF, down=False)
    k_up, v_dn, part, keep = tie((k_up, v_dn, part, keep))
    k_up, v_dn = tie((add(keep[1, :2], k_up), add(keep[2, 2:], v_dn)))
    k_up, v_dn = ring(k_up, False, 1), ring(v_dn, False, -1)
    v_up, k_dn = ring(keep[1, 2:], False, 1), ring(keep[2, :2], False, -1)
    part = swap(part)
    mine = weight_part(at, pieces, act, g, 0, F32)
    rest = weight_part(at, pieces, act, g, 1, BF, up=False)
    k_up, v_dn, v_up, k_dn, rest = tie((k_up, v_dn, v_up, k_dn, rest), mine)
    rest = swap(rest)
    total = jnp.concatenate([add(keep[0, :2], k_up, k_dn), add(keep[0, 2:], v_up, v_dn)], axis=0)
    parts = [ring(total[k], True, k) for k in (1, 3, 2)]
    gw_gate, gw_up, gw_down = weight_sum(at, mine, part, rest)
    parts = tie(parts, gw_gate)

    back = exchange(spread(at, [total[0], *parts], experts, slots))
    mine, other = combine(at, pick, back, experts, half)
    grad_tokens = (mine + swap(other)).astype(BF)
    return grad_tokens, gw_gate[None], gw_up[None], gw_down[None]


def solution(mesh):
    sizes = mesh.devices.shape
    fine = Mesh(
        mesh.devices.reshape(sizes[0], sizes[1], sizes[2] // 2, 2), ("dp", "expert", "x", "core")
    )
    by_token = P(("dp", "expert"), None)
    up = P("expert", None, ("dp", "x", "core"))
    down = P("expert", ("dp", "x", "core"), None)
    return jax.shard_map(
        shards,
        mesh=fine,
        in_specs=(by_token, by_token, by_token, by_token, up, up, down),
        out_specs=(P(("dp", "expert"), ("x", "core")), up, up, down),
        check_vma=False,
    )
```

```python
import jax
import jax.numpy as jnp
from jax import lax
from jax.experimental import pallas as pl
from jax.experimental.pallas import tpu as pltpu
from jax.sharding import Mesh, PartitionSpec as P

BF = jnp.bfloat16
F32 = jnp.float32
INSIDE = pl.BlockSpec(memory_space=pltpu.VMEM)
SCALARS = pl.BlockSpec(memory_space=pltpu.SMEM)


def swap(a):
    return lax.ppermute(a, "core", [(0, 1), (1, 0)])


def ring(a, second, step):
    nd, nx = lax.axis_size("dp"), lax.axis_size("x")
    pairs = []
    for d in range(nd):
        for x in range(nx):
            for c in range(2):
                along_x = (c == 0) != second
                to_d, to_x = (d, (x + step) % nx) if along_x else ((d + step) % nd, x)
                pairs.append(((d * nx + x) * 2 + c, (to_d * nx + to_x) * 2 + c))
    return lax.ppermute(a, ("dp", "x", "core"), pairs)


def dot(a, b, dims):
    return lax.dot_general(a, b, (dims, ((), ())), preferred_element_type=F32)


def add(*parts):
    out = parts[0].astype(F32)
    for p in parts[1:]:
        out = out + p.astype(F32)
    return out.astype(BF)


def tie(values, *late):
    out = lax.optimization_barrier((tuple(values), tuple(late)))
    return out[0]


def same(shape):
    return pl.BlockSpec(shape, lambda k, xi: (0,) * len(shape), pipeline_mode=pl.Buffered(1))


def call(body, grid, in_specs, out_specs, out_shape, args, flops, mib):
    return pl.pallas_call(
        body,
        grid_spec=pltpu.PrefetchScalarGridSpec(
            num_scalar_prefetch=1, grid=grid, in_specs=in_specs, out_specs=out_specs
        ),
        out_shape=out_shape,
        compiler_params=pltpu.CompilerParams(
            dimension_semantics=("arbitrary",), vmem_limit_bytes=mib << 20
        ),
        cost_estimate=pl.CostEstimate(flops=int(flops), bytes_accessed=8 << 20, transcendentals=0),
    )(*args)


def call_inside(body, out_specs, out_shape, args, flops, mib, scratch=()):
    return pl.pallas_call(
        body,
        in_specs=[SCALARS] + [INSIDE] * (len(args) - 1),
        out_specs=out_specs,
        out_shape=out_shape,
        scratch_shapes=scratch,
        compiler_params=pltpu.CompilerParams(vmem_limit_bytes=mib << 20),
        cost_estimate=pl.CostEstimate(flops=int(flops), bytes_accessed=8 << 20, transcendentals=0),
    )(*args)


def x_of(xi):
    return xi[0] // 2


def core_of(xi):
    return xi[0] % 2


def group_of(r, groups, size):
    g = jnp.zeros_like(r)
    for m in range(1, groups):
        g += (r >= m * size).astype(jnp.int32)
    return g


def dispatch(at, ids, gates, tokens, grad_out, half, slots, cols):
    experts = lax.axis_size("expert")
    every, rows = experts * slots, tokens.shape[0]

    def body(xi, ids, gates, tok, grad, sent, pick):
        j = lax.broadcasted_iota(jnp.int32, (every, 1), 0)
        e = group_of(j, experts, slots)
        j = j - e * slots
        is_x, is_y = j < half, (j >= half) & (j < 2 * half)
        s = jnp.where(is_x, j, j - half) + core_of(xi) * half
        first, second = ids[0:1, :] == e, ids[1:2, :] == e
        member = jnp.where(first | second, 1.0, 0.0)
        early = lax.broadcasted_iota(jnp.int32, (rows, rows), 0)
        late = lax.broadcasted_iota(jnp.int32, (rows, rows), 1)
        before = jnp.where(early < late, 1.0, 0.0).astype(BF)
        slot = dot(member.astype(BF), before, ((1,), (0,)))
        hit = jnp.where(slot == s.astype(F32), member, 0.0)
        hit_x, hit_y = jnp.where(is_x, hit, 0.0), jnp.where(is_y, hit, 0.0)
        gate = jnp.where(first, gates[0:1, :], 0.0) + jnp.where(second, gates[1:2, :], 0.0)
        gate = jnp.sum(hit_y * gate, axis=1, keepdims=True)
        hits = jnp.concatenate([hit_x, hit_y], axis=1).astype(BF)
        sources = jnp.concatenate([tok[...], grad[...]], axis=0)
        scale = jnp.where(is_y, gate, 1.0)
        sent[...] = (dot(hits, sources, ((1,), (0,))) * scale).astype(BF)
        pick[...] = (hit_x + hit_y).astype(BF)

    column = pl.BlockSpec((rows, cols), lambda k, xi: (0, x_of(xi)))
    return call(
        body,
        (1,),
        [same(ids.shape), same(gates.shape), column, column],
        [same((every, cols)), same((every, rows))],
        [jax.ShapeDtypeStruct((every, cols), BF), jax.ShapeDtypeStruct((every, rows), BF)],
        (at, ids, gates, tokens, grad_out),
        4 * every * rows * cols,
        56,
    )


def compact(at, got, experts, half):
    rows, cols = got.shape
    slots = rows // experts
    side = experts * half

    def body(xi, a, out):
        r = lax.broadcasted_iota(jnp.int32, (2 * side, 1), 0)
        is_y = (r >= side).astype(jnp.int32)
        r = r - is_y * side
        e = group_of(r, experts, half)
        place = e * slots + is_y * half + r - e * half
        q = lax.broadcasted_iota(jnp.int32, (2 * side, rows), 1)
        m = jnp.where(q == place, 1.0, 0.0).astype(BF)
        out[...] = dot(m, a[...], ((1,), (0,))).astype(BF)

    return call_inside(
        body,
        INSIDE,
        jax.ShapeDtypeStruct((2 * side, cols), BF),
        (at, got),
        4 * side * rows * cols,
        8,
    )


def spread(at, parts, experts, slots):
    side, cols = parts[0].shape
    half = side // experts
    rows = experts * slots

    def body(xi, *refs):
        *ins, out = refs
        total = ins[0][...].astype(F32)
        for a in ins[1:]:
            total += a[...].astype(F32)
        total = total.astype(BF)
        j = lax.broadcasted_iota(jnp.int32, (rows, 1), 0)
        e = group_of(j, experts, slots)
        j = j - e * slots
        q = lax.broadcasted_iota(jnp.int32, (rows, side), 1)
        low = jnp.where((q == e * half + j) & (j < half), 1.0, 0.0).astype(BF)
        high = (q == e * half + j - half) & (j >= half) & (j < 2 * half)
        high = jnp.where(high, 1.0, 0.0).astype(BF)
        out[...] = (
            dot(low, total[:, : cols // 2], ((1,), (0,)))
            + dot(high, total[:, cols // 2 :], ((1,), (0,)))
        ).astype(BF)

    return call_inside(
        body,
        INSIDE,
        jax.ShapeDtypeStruct((rows, cols // 2), BF),
        (at, *parts),
        2 * rows * side * cols,
        8,
    )


def combine(at, pick, back, experts, half):
    rows, tokens = pick.shape
    cols = back.shape[1]
    slots = rows // experts

    def body(xi, pick, back, mine, other):
        j = lax.broadcasted_iota(jnp.int32, (rows, 1), 0)
        j = j - group_of(j, experts, slots) * slots
        a = back[...]
        none = jnp.zeros_like(a)
        low = dot(pick[...], jnp.where(j < half, a, none), ((0,), (0,)))
        high = dot(pick[...], jnp.where(j >= half, a, none), ((0,), (0,)))
        on0 = core_of(xi) == 0
        mine[...] = jnp.where(on0, low, high)
        other[...] = jnp.where(on0, high, low)

    shape = jax.ShapeDtypeStruct((tokens, cols), F32)
    return call_inside(
        body, [INSIDE] * 2, [shape] * 2, (at, pick, back), 4 * rows * tokens * cols, 8
    )


def pack(at, own, theirs):
    width, hid = own[0].shape
    cols = width // 4
    up = pl.BlockSpec((cols, hid), lambda k, xi: ((x_of(xi) + k) % 4, 0))
    down = pl.BlockSpec((hid, cols), lambda k, xi: (0, (x_of(xi) + k) % 4))

    def body(xi, g1, u1, d1, g2, u2, d2, w, wd):
        for j, ref in enumerate((g1, u1, g2, u2)):
            w[0, :, j * hid : (j + 1) * hid] = ref[...]
        wd[0, :hid] = d1[...]
        wd[0, hid:] = d2[...]

    return call(
        body,
        (4,),
        [up, up, down] * 2,
        [
            pl.BlockSpec((1, cols, 4 * hid), lambda k, xi: (k, 0, 0)),
            pl.BlockSpec((1, 2 * hid, cols), lambda k, xi: (k, 0, 0)),
        ],
        [
            jax.ShapeDtypeStruct((4, cols, 4 * hid), BF),
            jax.ShapeDtypeStruct((4, 2 * hid, cols), BF),
        ],
        (at, *own, *theirs),
        width * hid,
        14,
    )


def put_in(xi, hu, ga, piece, first, s, w, wd):
    on0 = core_of(xi) == 0
    row, col = jnp.where(on0, s, first), jnp.where(on0, first, s)
    rows = hu.shape[1]
    hu[row] += dot(piece[:rows], w[col], ((1,), (0,)))
    ga[row] += dot(piece[rows:], wd[col], ((1,), (1,)))


def early_part(at, pieces, places, w, wd, so_far=None):
    n = len(pieces)
    rows = pieces[0].shape[1] // 2
    count = pieces[0].shape[0]
    more = [] if so_far is None else list(so_far)

    def body(xi, *refs):
        ps, w, wd, hu, ga = refs[:n], refs[n], refs[n + 1], refs[-2], refs[-1]
        if more:
            hu[...] = refs[n + 2][...]
            ga[...] = refs[n + 3][...]
        else:
            hu[...] = jnp.zeros_like(hu)
            ga[...] = jnp.zeros_like(ga)

        @pl.loop(0, count)
        def _(k):
            for p, (first, s) in zip(ps, places):
                put_in(xi, hu, ga, p.at[k], first + k, s, w, wd)

    shapes = [
        jax.ShapeDtypeStruct((4, rows, w.shape[2]), F32),
        jax.ShapeDtypeStruct((4, rows, wd.shape[1]), F32),
    ]
    return call_inside(
        body,
        [INSIDE] * 2,
        shapes,
        (at, *pieces, w, wd, *more),
        2 * n * count * rows * w.shape[1] * (w.shape[2] + wd.shape[1]),
        12,
    )


def token_part(at, hu, ga, p2a, p2b, w, wd):
    rows = hu.shape[1]
    cols = w.shape[1]
    hid = w.shape[2] // 4
    every = 4 * rows

    def body(xi, hu, ga, pa, pb, w, wd, act, g, keep):
        def finish(k, hu2, ga2):
            r = slice(k * rows, (k + 1) * rows)
            for c in range(2):
                part = slice(c * hid, (c + 1) * hid)
                hs = slice(2 * c * hid, (2 * c + 1) * hid)
                us = slice((2 * c + 1) * hid, (2 * c + 2) * hid)
                hh, uu, gg = hu[k, :, hs], hu[k, :, us], ga[k, :, part]
                if hu2 is not None:
                    hh, uu, gg = hh + hu2[:, hs], uu + hu2[:, us], gg + ga2[:, part]
                s = jax.nn.sigmoid(hh)
                silu = hh * s
                act[r, part] = (silu * uu).astype(BF)
                g[r, hs] = (gg * uu * (s * (1.0 + hh * (1.0 - s)))).astype(BF)
                g[r, us] = (gg * silu).astype(BF)

        last = ((pa, 0), (pa, 1), (pb, 0), (pb, 1))

        @pl.when(core_of(xi) == 0)
        def _():
            hu2 = ga2 = 0.0
            for k, (p, n) in enumerate(last):
                hu2 += dot(p[n, :rows], w[k], ((1,), (0,)))
                ga2 += dot(p[n, rows:], wd[k], ((1,), (1,)))
            for k in range(4):
                finish(k, *((hu2, ga2) if k == 2 else (None, None)))

        @pl.when(core_of(xi) == 1)
        def _():
            x = jnp.concatenate([p[n, :rows] for p, n in last], axis=0)
            y = jnp.concatenate([p[n, rows:] for p, n in last], axis=0)
            hu2 = dot(x, w[2], ((1,), (0,)))
            ga2 = dot(y, wd[2], ((1,), (1,)))
            for k in range(4):
                r = slice(k * rows, (k + 1) * rows)
                finish(k, hu2[r], ga2[r])

        @pl.when(core_of(xi) == 0)
        def _():
            out = dot(g[...], w[2], ((1,), (1,))).astype(BF)
            for j in range(4):
                keep[j] = out[j * rows : (j + 1) * rows]

        @pl.when(core_of(xi) == 1)
        def _():
            mine = g[2 * rows : 3 * rows]
            for k in range(4):
                keep[k] = dot(mine, w[k], ((1,), (1,))).astype(BF)

    return call_inside(
        body,
        [INSIDE] * 3,
        [
            jax.ShapeDtypeStruct((every, 2 * hid), BF),
            jax.ShapeDtypeStruct((every, 4 * hid), BF),
            jax.ShapeDtypeStruct((4, rows, cols), BF),
        ],
        (at, hu, ga, p2a, p2b, w, wd),
        every * 4 * cols * 4 * hid,
        20,
    )


def other_blocks(at, g, w):
    cols = w.shape[1]
    rows = g.shape[0] // 4
    places = (0, 1, 3)

    def body(xi, g, w, keep):
        @pl.when(core_of(xi) == 0)
        def _():
            for n, k in enumerate(places):
                out = dot(g[...], w[k], ((1,), (1,))).astype(BF)
                for j in range(4):
                    keep[n, j] = out[j * rows : (j + 1) * rows]

        @pl.when(core_of(xi) == 1)
        def _():
            mine = jnp.concatenate([g[: 2 * rows], g[3 * rows :]], axis=0)

            @pl.loop(0, 4)
            def _(k):
                out = dot(mine, w[k], ((1,), (1,))).astype(BF)
                for n in range(3):
                    keep[n, k] = out[n * rows : (n + 1) * rows]

    return call_inside(
        body,
        INSIDE,
        jax.ShapeDtypeStruct((3, 4, rows, cols), BF),
        (at, g, w),
        2 * 3 * rows * 4 * cols * w.shape[2],
        12,
    )


def weight_part(at, pieces, act, g, which, dtype, up=True, down=True):
    p0 = pieces[0]
    rows, cols = p0.shape[1] // 2, p0.shape[2]
    every, width = 4 * rows, 4 * cols
    hid = act.shape[1] // 2
    squares = [slice(j * hid, (j + 1) * hid) for j in range(cols // hid)]
    size = (2 * up + down) * hid

    def body(xi, p0, p1a, p1b, p2a, p2b, p3a, p3b, act, g, *refs):
        xbuf, ybuf = refs[-2:]

        def load(sources):
            for j, (ref, n) in enumerate(sources):
                if up:
                    xbuf[j * rows : (j + 1) * rows] = ref[n, :rows]
                if down:
                    ybuf[j * rows : (j + 1) * rows] = ref[n, rows:]

        def step(k):
            on0 = core_of(xi) == 0

            @pl.when(on0 & (k < 2))
            def _():
                load([(p0, k), (p1a, k), (p2a, k), (p3a, k)])

            @pl.when(on0 & (k >= 2))
            def _():
                load([(p0, k), (p1b, k - 2), (p2b, k - 2), (p3b, k - 2)])

            for n, (a, b) in enumerate(((p0, p0), (p1a, p1b), (p2a, p2b), (p3a, p3b))):

                @pl.when(jnp.logical_not(on0) & (k == n))
                def _():
                    shift = 2 if a is b else 0
                    load([(a, 0), (a, 1), (b, shift), (b, shift + 1)])

            cut = slice(which * hid, (which + 1) * hid)
            cut2 = slice(2 * which * hid, 2 * (which + 1) * hid)
            return (
                dot(xbuf[...], g[:, cut2], ((0,), (0,))) if up else None,
                dot(act[:, cut], ybuf[...], ((0,), (0,))) if down else None,
            )

        out = refs[0]

        @pl.loop(0, 4)
        def _(k):
            for_up, for_down = step(k)
            if up:
                out[k, :, : 2 * hid] = for_up.astype(out.dtype)
            if down:
                for c in squares:
                    out[k, c, size - hid :] = for_down[:, c].astype(out.dtype)

    return call_inside(
        body,
        INSIDE,
        jax.ShapeDtypeStruct((4, cols, size), dtype),
        (at, *pieces, act, g),
        2 * every * width * size,
        14,
        [pltpu.VMEM((every, cols), BF)] * 2,
    )


def weight_sum(at, mine, other_up, other_down):
    _, cols, hid = mine.shape
    hid //= 3
    width = 4 * cols

    def body(xi, mine, up, down, og, ou, od, sg, su, sd, sems):
        def copies(k):
            block = pl.ds(pl.multiple_of((x_of(xi) + k) % 4 * cols, cols), cols)
            return (
                pltpu.make_async_copy(sg.at[k], og.at[block, :], sems.at[k, 0]),
                pltpu.make_async_copy(su.at[k], ou.at[block, :], sems.at[k, 1]),
                pltpu.make_async_copy(sd.at[k], od.at[:, block], sems.at[k, 2]),
            )

        @pl.loop(0, 4)
        def _(k):
            total = (mine[k, :, : 2 * hid] + up[k].astype(F32)).astype(BF)
            sg[k] = total[:, :hid]
            su[k] = total[:, hid:]
            total = (mine[k, :, 2 * hid :] + down[k].astype(F32)).astype(BF)
            for j in range(cols // hid):
                c = slice(j * hid, (j + 1) * hid)
                sd[k, :, c] = total[c]
            for copy in copies(k):
                copy.start()

        @pl.loop(0, 4)
        def _(k):
            for copy in copies(k):
                copy.wait()

    return call_inside(
        body,
        [pl.BlockSpec(memory_space=pl.ANY)] * 3,
        [
            jax.ShapeDtypeStruct((width, hid), BF),
            jax.ShapeDtypeStruct((width, hid), BF),
            jax.ShapeDtypeStruct((hid, width), BF),
        ],
        (at, mine, other_up, other_down),
        12 * width * hid,
        14,
        [
            pltpu.VMEM((4, cols, hid), BF),
            pltpu.VMEM((4, cols, hid), BF),
            pltpu.VMEM((4, hid, cols), BF),
            pltpu.SemaphoreType.DMA((4, 3)),
        ],
    )


def shards(tokens, grad_out, gate_prob, expert_ids, w_gate, w_up, w_down):
    rows, width = tokens.shape
    experts = lax.axis_size("expert")
    capacity = rows * 9 // (4 * experts)
    half = capacity // 2
    cols = width // lax.axis_size("x")
    slots = (capacity + 7) // 8 * 8
    at = lax.axis_index(("x", "core")).astype(jnp.int32).reshape(1)
    own = (w_gate[0], w_up[0], w_down[0])
    theirs = [swap(w) for w in own]

    def exchange(a):
        a = a.reshape(experts, slots, -1)
        a = lax.all_to_all(a, "expert", split_axis=0, concat_axis=0, tiled=True)
        return a.reshape(experts * slots, -1)

    sent, pick = dispatch(at, expert_ids.T, gate_prob.T, tokens, grad_out, half, slots, cols)
    (got,) = tie((exchange(sent),), *theirs)
    got = compact(at, got, experts, half)
    w, wd = pack(at, own, theirs)

    f1, f3, f2 = ring(got, False, -1), ring(got, False, 1), ring(got, False, 2)
    p0 = jnp.stack([got, f1, f2, f3])
    p1a, p3b = ring(p0[:2], True, -1), ring(p0[2:], True, 1)
    p1b, p3a = ring(p0[2:], True, -1), ring(p0[:2], True, 1)
    early = early_part(at, (p0,), ((0, 0),), w, wd)
    p1a, p3b = tie((p1a, p3b), *early)
    p2a, p2b = ring(p1a, True, -1), ring(p3b, True, 1)
    places = ((0, 1), (2, 1), (0, 3), (2, 3))
    hu, ga = early_part(at, (p1a, p1b, p3a, p3b), places, w, wd, early)
    p2a, p2b = tie((p2a, p2b), hu, ga)
    act, g, first = token_part(at, hu, ga, p2a, p2b, w, wd)
    pieces = (p0, p1a, p1b, p2a, p2b, p3a, p3b)

    k_up, v_dn = ring(first[:2], False, 1), ring(first[2:], False, -1)
    keep = other_blocks(at, g, w)
    part = weight_part(at, pieces, act, g, 1, BF, down=False)
    k_up, v_dn, part, keep = tie((k_up, v_dn, part, keep))
    k_up, v_dn = tie((add(keep[1, :2], k_up), add(keep[2, 2:], v_dn)))
    k_up, v_dn = ring(k_up, False, 1), ring(v_dn, False, -1)
    v_up, k_dn = ring(keep[1, 2:], False, 1), ring(keep[2, :2], False, -1)
    part = swap(part)
    mine = weight_part(at, pieces, act, g, 0, F32)
    rest = weight_part(at, pieces, act, g, 1, BF, up=False)
    k_up, v_dn, v_up, k_dn, rest = tie((k_up, v_dn, v_up, k_dn, rest), mine)
    rest = swap(rest)
    total = jnp.concatenate([add(keep[0, :2], k_up, k_dn), add(keep[0, 2:], v_up, v_dn)], axis=0)
    parts = [ring(total[k], True, k) for k in (1, 3, 2)]
    gw_gate, gw_up, gw_down = weight_sum(at, mine, part, rest)
    parts = tie(parts, gw_gate)

    back = exchange(spread(at, [total[0], *parts], experts, slots))
    mine, other = combine(at, pick, back, experts, half)
    grad_tokens = (mine + swap(other)).astype(BF)
    return grad_tokens, gw_gate[None], gw_up[None], gw_down[None]


def solution(mesh):
    sizes = mesh.devices.shape
    fine = Mesh(
        mesh.devices.reshape(sizes[0], sizes[1], sizes[2] // 2, 2), ("dp", "expert", "x", "core")
    )
    by_token = P(("dp", "expert"), None)
    up = P("expert", None, ("dp", "x", "core"))
    down = P("expert", ("dp", "x", "core"), None)
    return jax.shard_map(
        shards,
        mesh=fine,
        in_specs=(by_token, by_token, by_token, by_token, up, up, down),
        out_specs=(P(("dp", "expert"), ("x", "core")), up, up, down),
        check_vma=False,
    )
```
